256 devices in a mesh: ctx: 8 (over z), head: 32 (over x, y, core).
Axes of the slice: x: 4, y: 4, z: 8, core: 2. Of those that a mesh axis runs over, the one named last changes fastest.
Arguments:
- query_raw: bfloat16 [16384, 2048], P(('ctx', 'head')), may hold values from -6 to 6
- key_raw: bfloat16 [16384, 2048], P(('ctx', 'head')), may hold values from -6 to 6
- value_raw: bfloat16 [16384, 4096], P(('ctx', 'head')), may hold values from -6 to 6
- decay_raw: bfloat16 [16384, 32], P(('ctx', 'head'))
- beta_raw: bfloat16 [16384, 32], P(('ctx', 'head'))
- decay_base: float32 [32], replicated
- decay_bias: float32 [32], replicated, may hold values from -0.5 to 0.5
- doc_lengths: int32 [4], replicated, may hold values from 1 to 8192, 16384 in all
- out_grad: bfloat16 [16384, 4096], P(('ctx', 'head')), may hold values from -6 to 6
Outputs:
- output: bfloat16 [16384, 4096], P(('ctx', 'head'))
- query_grad: bfloat16 [16384, 2048], P(('ctx', 'head'))
- key_grad: bfloat16 [16384, 2048], P(('ctx', 'head'))
- value_grad: bfloat16 [16384, 4096], P(('ctx', 'head'))
- decay_grad: bfloat16 [16384, 32], P(('ctx', 'head'))
- beta_grad: bfloat16 [16384, 32], P(('ctx', 'head'))
The draws below stay inside these ranges and needn't reach their ends.
All inputs are finite; a program needn't handle non-finite values.
Results may differ from the reference program's by a relative error of at most 0.02.
Values may be sent and summed in bfloat16 or wider, within the bound.
No kernel may reach another device: no remote copies, remote signals or barrier semaphores. Data moves between devices by JAX's collectives and lax.ppermute only.
A program may use at most 128 MiB of HBM per device.

```python
import math
import jax
import jax.numpy as jnp
import numpy as np
from jax import lax

VALUE_HEAD_COUNT = 32
NK = 16
DK = 128
DV = 128
GROUP = 128
NDOC = 4
WINDOW_TOKENS = 16384


def gate_plan(key, slow_count):
    plan_key = jax.random.fold_in(key, 7)
    order_key, rate_key = jax.random.split(plan_key, 2)
    order = jax.random.permutation(order_key, VALUE_HEAD_COUNT)
    is_slow = order < slow_count
    spread = jax.random.uniform(rate_key, (VALUE_HEAD_COUNT,), jnp.float32)
    slow_rate = jnp.exp(jnp.log(0.025 / WINDOW_TOKENS) + spread * jnp.log(16.0))
    fast_rate = jnp.exp(jnp.log(0.02) + spread * jnp.log(5.0))
    return (jnp.log(jnp.where(is_slow, slow_rate, fast_rate)), is_slow)


def draw_decay_base(key, part):
    slow_count = VALUE_HEAD_COUNT // 2
    return gate_plan(key, slow_count)[0].astype(jnp.float32)


def draw_beta_raw(key, part):
    slow_count = VALUE_HEAD_COUNT // 2
    is_slow = gate_plan(key, slow_count)[1]
    key = jax.random.fold_in(key, 13)
    fast_random_key, slow_random_key = jax.random.split(key, 2)
    fast_values = jnp.clip(1.5 * jax.random.normal(fast_random_key, (WINDOW_TOKENS, VALUE_HEAD_COUNT), jnp.float32), -6.0, 6.0)
    slow_values = jnp.clip(-4.0 + 0.5 * jax.random.normal(slow_random_key, (WINDOW_TOKENS, VALUE_HEAD_COUNT), jnp.float32), -5.5, -2.5)
    return jnp.where(is_slow[None, :], slow_values, fast_values).astype(jnp.bfloat16)


def draw_decay_raw(key, part):
    slow_count = VALUE_HEAD_COUNT // 2
    decay_rates = jnp.exp(gate_plan(key, slow_count)[0])
    spike_random_key = jax.random.fold_in(key, 11)
    root_random_key, location_random_key, objective_random_key = jax.random.split(spike_random_key, 3)
    spike_count = 3
    base_values = jax.random.uniform(root_random_key, (WINDOW_TOKENS, VALUE_HEAD_COUNT), jnp.float32, -2.0, 2.0)
    spike_locations = jax.random.randint(location_random_key, (spike_count, VALUE_HEAD_COUNT), 0, WINDOW_TOKENS)
    objective_values = jax.random.uniform(objective_random_key, (spike_count, VALUE_HEAD_COUNT), jnp.float32, 0.2, 0.5)
    spike_values = -jnp.log(1.0 - objective_values) / decay_rates[None, :]
    matched_entries = jnp.arange(WINDOW_TOKENS)[:, None, None] == spike_locations[None, :, :]
    selected_entries = jnp.max(jnp.where(matched_entries, spike_values[None, :, :], -1e+30), axis=1)
    struck = jnp.any(matched_entries, axis=1)
    return jnp.where(struck, selected_entries, base_values).astype(jnp.bfloat16)


def level_of(rng, extent, cuts, low, largest):
    loudness, own = 1.0, jax.random.fold_in(rng, 6)
    for dim, blocks in cuts:
        heights = jnp.exp(jax.random.uniform(jax.random.fold_in(own, dim), (blocks,), jnp.float32, low / len(cuts), largest / len(cuts)))
        loudness = loudness * jnp.repeat(heights, extent[dim] // blocks).reshape([-1 if axis == dim else 1 for axis in range(len(extent))])
    return loudness


def split_up(number_of, total, most, slope):
    loads = [(1 << 20) // math.isqrt(grade ** slope) + 1 for grade in range(2, number_of + 1)]
    rest, counts = total - most - (number_of - 1), [1] * (number_of - 1)
    while rest > 0:
        movable = [i for i in range(number_of - 1) if counts[i] < most]
        mass, budget = sum([loads[i] for i in movable]), rest
        for i in movable:
            more = min(most - counts[i], max(1, budget * loads[i] // mass), rest)
            counts[i] = counts[i] + more
            rest = rest - more
    return np.array([most] + counts)


def ragged(key, amount, total, most, slope):
    if amount == 2:
        one = jax.random.randint(key, (), max(1, total - most), min(most, total - 1) + 1)
        return jnp.stack([one, total - one])
    lengths = jnp.asarray(split_up(amount, total, most, slope), jnp.int32)
    twos = (amount - 1) // 2
    donor, taker = lengths[1:1 + 2 * twos:2], lengths[2:2 + 2 * twos:2]
    margin = jnp.minimum(donor - 1, most - taker)
    moved = jax.random.randint(jax.random.fold_in(key, 1), (twos,), 0, 1 << 20) % (margin + 1)
    lengths = lengths.at[1:1 + 2 * twos:2].set(donor - moved).at[2:2 + 2 * twos:2].set(taker + moved)
    return lengths[jax.random.permutation(jax.random.fold_in(key, 2), amount)]


def centred(rng, dims, scale, bound, shards=(), held_as=jnp.bfloat16):
    entries = jax.random.normal(rng, dims, jnp.float32) * scale
    if len(shards) > 0:
        entries = level_of(rng, dims, shards, -0.22, 0.18) * entries
    return jnp.clip(entries, min=-bound, max=bound).astype(held_as)


def setup_inputs(seed: int = 0) -> dict:
    streams_of = jax.random.split(jax.random.key(seed), 10)
    query_raw = centred(streams_of[0], (WINDOW_TOKENS, NK * DK), 1.0, 6.0, ((0, 256),))
    key_raw = centred(streams_of[1], (WINDOW_TOKENS, NK * DK), 1.0, 6.0, ((0, 256),))
    value_raw = centred(streams_of[2], (WINDOW_TOKENS, VALUE_HEAD_COUNT * DV), 1.0, 6.0, ((0, 256),))
    decay_raw = draw_decay_raw(jax.random.fold_in(streams_of[9], 71), 0)
    beta_raw = draw_beta_raw(jax.random.fold_in(streams_of[9], 71), 0)
    decay_base = draw_decay_base(jax.random.fold_in(streams_of[9], 71), 0)
    decay_bias = jnp.clip(jax.random.uniform(streams_of[6], (VALUE_HEAD_COUNT,), jnp.float32, -0.5, 0.5), -0.5, 0.5)
    doc_lengths = ragged(streams_of[7], NDOC, WINDOW_TOKENS, WINDOW_TOKENS // 2, 2).astype(jnp.int32)
    out_grad = centred(streams_of[8], (WINDOW_TOKENS, VALUE_HEAD_COUNT * DV), 1.0, 6.0, ((0, 256),))
    return {"query_raw": query_raw, "key_raw": key_raw, "value_raw": value_raw, "decay_raw": decay_raw, "beta_raw": beta_raw, "decay_base": decay_base, "decay_bias": decay_bias, "doc_lengths": doc_lengths, "out_grad": out_grad}


precise = lax.Precision.HIGHEST

def product(left, right):
    return jnp.matmul(left, right, precision=precise)

def low_product(left, right):
    return jnp.matmul(left.astype(jnp.bfloat16), right.astype(jnp.bfloat16), preferred_element_type=jnp.float32)

def swap_last(matrix):
    return jnp.swapaxes(matrix, -1, -2)

def segment_of(doc_lengths, positions):
    starts = jnp.cumsum(doc_lengths) - doc_lengths
    inside = (positions[:, None] >= starts[None, :]).astype(jnp.int32)
    return lax.optimization_barrier(jnp.sum(inside, axis=1)) - 1

def unit_norm(vectors):
    return vectors * lax.rsqrt(lax.optimization_barrier(jnp.sum(vectors * vectors, axis=-1, keepdims=True)) + 1e-06)

def gate_terms(query_raw, key_raw, decay_raw, beta_raw, decay_base, decay_bias):
    query = unit_norm(query_raw) * query_raw.shape[-1] ** (-0.5)
    keys_unit = unit_norm(key_raw)
    decay_log = -jnp.exp(decay_base) * jax.nn.softplus(decay_raw + decay_bias)
    beta_gate = jax.nn.sigmoid(beta_raw)
    return (query, keys_unit, decay_log, beta_gate)

def group_tables(query, keys_unit, decay_log, beta_gate, segment, before):
    group_span = decay_log.shape[-1]
    cumulative = jnp.cumsum(decay_log, axis=-1)
    indices = jnp.arange(group_span)
    lower_mask = indices[:, None] >= indices[None, :]
    strict_mask = indices[:, None] > indices[None, :]
    joined = lower_mask & (segment[..., :, None] == segment[..., None, :])
    spread = cumulative[..., :, None] - cumulative[..., None, :]
    decay_table = jnp.where(joined, jnp.exp(jnp.where(joined, spread, 0.0)), 0.0)
    entry_decay = jnp.where(segment == before[..., None], jnp.exp(cumulative), 0.0)
    weighted = decay_table * beta_gate[..., None, :]
    nilpotent = -jnp.where(strict_mask, weighted * low_product(keys_unit, swap_last(keys_unit)), 0.0)
    inverse = jnp.eye(group_span, dtype=jnp.float32) + nilpotent
    powered = nilpotent
    for doubling in range((group_span - 1).bit_length() - 1):
        powered = product(powered, powered)
        inverse = inverse + product(inverse, powered)
    mixing = weighted * low_product(query, swap_last(keys_unit))
    return (inverse, mixing, entry_decay, weighted[..., -1, :])

def group_step(carried, tables):
    inverse, mixing, entry_decay, last_weight, query, keys_unit, values = tables
    pushed = values - entry_decay[:, None] * low_product(keys_unit, carried)
    fresh_values = product(inverse, pushed)
    output = entry_decay[:, None] * low_product(query, carried) + low_product(mixing, fresh_values)
    carried = entry_decay[-1] * carried + low_product(swap_last(keys_unit), last_weight[:, None] * fresh_values)
    return (carried, output)

def head_run(query, keys_unit, values, decay_log, beta_gate, segment, before, carried):
    blocks = query.shape[0] // GROUP

    def split_blocks(member):
        return member.reshape((blocks, GROUP) + member.shape[1:])
    pieces = [split_blocks(member) for member in (query, keys_unit, values, decay_log, beta_gate, segment)]
    tables = group_tables(pieces[0], pieces[1], pieces[3], pieces[4], pieces[5], before)
    carried, outputs = lax.scan(group_step, carried, tables + (pieces[0], pieces[1], pieces[2]))
    return (outputs.reshape((-1, values.shape[-1])), carried)

def reference(query_raw, key_raw, value_raw, decay_raw, beta_raw, decay_base, decay_bias, doc_lengths, out_grad):
    length_total = query_raw.shape[0]
    repeat_count = VALUE_HEAD_COUNT // NK
    positions = jnp.arange(length_total, dtype=jnp.int32)
    segment = segment_of(doc_lengths, positions)
    before = segment_of(doc_lengths, positions[::GROUP] - 1)

    def by_head(matrix, width_head, repeats):
        heads_first = jnp.moveaxis(matrix.astype(jnp.float32).reshape(length_total, -1, width_head), 1, 0)
        return jnp.repeat(heads_first, repeats, axis=0)
    query_heads = by_head(query_raw, DK, repeat_count)
    key_heads = by_head(key_raw, DK, repeat_count)
    value_heads = by_head(value_raw, DV, 1)
    grad_heads = by_head(out_grad, DV, 1)
    decay_heads = decay_raw.astype(jnp.float32).T
    beta_heads = beta_raw.astype(jnp.float32).T

    def one_head(items):
        head_query, head_key, head_value, head_decay, head_beta, head_base, head_bias, head_grad = items

        def forward(query_part, key_part, value_part, decay_part, beta_part):
            query, keys_unit, decay_log, beta_gate = gate_terms(query_part, key_part, decay_part, beta_part, head_base, head_bias)
            outputs, carried = head_run(query, keys_unit, value_part, decay_log, beta_gate, segment, before, jnp.zeros((DK, DV), jnp.float32))
            return outputs
        outputs, pullback = jax.vjp(forward, head_query, head_key, head_value, head_decay, head_beta)
        return (outputs,) + tuple(pullback(head_grad))
    results = lax.map(one_head, (query_heads, key_heads, value_heads, decay_heads, beta_heads, decay_base, decay_bias, grad_heads))
    outputs, query_grads, key_grads, value_grads, decay_grads, beta_grads = results

    def to_rows(heads):
        return jnp.moveaxis(heads, 0, 1).reshape(length_total, -1)

    def pair_sum(heads):
        rounded = lax.optimization_barrier(heads.astype(jnp.bfloat16)).astype(jnp.float32)
        summed = lax.optimization_barrier(jnp.sum(rounded.reshape((NK, repeat_count) + heads.shape[1:]), axis=1))
        return to_rows(summed).astype(jnp.bfloat16)
    return (to_rows(outputs).astype(jnp.bfloat16), pair_sum(query_grads), pair_sum(key_grads), to_rows(value_grads).astype(jnp.bfloat16), decay_grads.T.astype(jnp.bfloat16), beta_grads.T.astype(jnp.bfloat16))
```

```python
import functools

import jax
import jax.numpy as jnp
from jax import lax
from jax.experimental import pallas as pl
from jax.experimental.pallas import tpu as pltpu
from jax.sharding import PartitionSpec as P

VALUE_HEAD_COUNT = 32
NK = 16
DK = 128
DV = 128
GROUP = 128
GATE_ROWS = 16
STEP_BLOCKS = 4
VMEM_BYTES = 60 * 1024 * 1024

bf16 = jnp.bfloat16
f32 = jnp.float32


def contract(left, right, left_dim, right_dim):
    return lax.dot_general(
        left.astype(bf16),
        right.astype(bf16),
        (((left_dim,), (right_dim,)), ((), ())),
        preferred_element_type=f32,
    )


def mm(left, right):
    return contract(left, right, 1, 0)


def mm_nt(left, right):
    return contract(left, right, 1, 1)


def mm_tn(left, right):
    return contract(left, right, 0, 0)


def exact(left, right, left_dim, right_dim):
    return lax.dot_general(
        left,
        right,
        (((left_dim,), (right_dim,)), ((), ())),
        preferred_element_type=f32,
        precision=lax.Precision.HIGHEST,
    )


def iota(shape, dim):
    return lax.broadcasted_iota(jnp.int32, shape, dim)


def segment_of(positions, starts):
    count = jnp.zeros(positions.shape, jnp.int32)
    for start in starts:
        count = count + jnp.where(positions >= start, 1, 0)
    return count


def pick_column(table, block):
    lane = iota(table.shape, 1)
    return jnp.sum(jnp.where(lane == block, table, 0.0), axis=1, keepdims=True)


def block_gates(block, ints_ref, gate_ref, column_ref):
    starts = [ints_ref[1 + j] for j in range(4)]
    first = ints_ref[0] * 16 * GROUP + block * GROUP
    cum_row = gate_ref[0, pl.ds(block, 1), :]
    beta_row = gate_ref[1, pl.ds(block, 1), :]
    cum_col = pick_column(column_ref[0], block)
    beta_col = pick_column(column_ref[1], block)
    seg_row = segment_of(first + iota((1, GROUP), 1), starts)
    seg_col = segment_of(first + iota((GROUP, 1), 0), starts)
    before = segment_of(jnp.full((1, 1), first - 1, jnp.int32), starts)
    row, col = iota((GROUP, GROUP), 0), iota((GROUP, GROUP), 1)
    joined = (row >= col) & (seg_col == seg_row)
    spread = jnp.where(joined, cum_col - cum_row, 0.0)
    weighted = jnp.where(joined, jnp.exp(spread), 0.0) * beta_row
    entry = jnp.where(seg_col == before, jnp.exp(cum_col), 0.0)
    cum_last = cum_col[GROUP - 1 :, :]
    same_last = seg_col == seg_col[GROUP - 1 :, :]
    last = (
        jnp.where(same_last, jnp.exp(jnp.where(same_last, cum_last - cum_col, 0.0)), 0.0) * beta_col
    )
    return weighted, entry, last, row, col


def inverse_root(raw):
    return lax.rsqrt(jnp.sum(raw * raw, axis=1, keepdims=True) + 1e-06)


def block_rows(x_ref, local, part):
    return jnp.concatenate(
        [x_ref[2 * local + half, 64 * part : 64 * part + 64, :] for half in range(2)], axis=0
    )


def normed(x_ref, local):
    query_raw = block_rows(x_ref, local, 0).astype(f32)
    key_raw = block_rows(x_ref, local, 1).astype(f32)
    query_root, key_root = inverse_root(query_raw), inverse_root(key_raw)
    query = query_raw * query_root * DK ** (-0.5)
    keys = key_raw * key_root
    return query_raw, key_raw, query_root, key_root, query.astype(bf16), keys.astype(bf16)


def triangular_inverse(strict, row, col):
    differ = row ^ col
    eye = jnp.where(differ == 0, 1.0, 0.0)
    inverse = eye - jnp.where(differ == 1, strict, 0.0)
    for level in range(1, 7):
        size = 1 << level
        between = jnp.where((differ >= size) & (differ < 2 * size), strict, 0.0).astype(bf16)
        held = inverse.astype(bf16)
        inverse = inverse - mm(mm(held, between), held)
    held = inverse.astype(bf16)
    upper = strict.astype(bf16)
    lower = (strict - upper.astype(f32)).astype(bf16)
    rest = eye - held.astype(f32) - mm(upper, held) - mm(lower, held)
    return held.astype(f32) + mm(held, rest)


def tables_kernel(
    ints_ref,
    floats_ref,
    gates_in_ref,
    x_ref,
    send_ref,
    gate_ref,
    column_ref,
    fresh_ref,
    out_ref,
    push_ref,
    maps_ref,
    prefix_ref,
    prefix_free_ref,
    suffix_ref,
    suffix_free_ref,
    step_ref,
    term_ref,
    carry_ref,
):
    here = pl.program_id(0)

    @pl.when(here == 0)
    def prologue():
        tail = gates_in_ref[...].astype(f32)
        paired = tail.reshape(16, 2, GATE_ROWS, 128)
        lane = iota((16, GATE_ROWS, 128), 2)
        rows = iota((16, GATE_ROWS, 128), 1)
        tail = jnp.where(lane < 64, paired[:, 0], paired[:, 1])
        decay_raw = jnp.sum(jnp.where(rows == 0, tail, 0.0), axis=1) + floats_ref[1]
        beta_raw = jnp.sum(jnp.where(rows == 1, tail, 0.0), axis=1)
        rate = -jnp.exp(jnp.full((16, 128), floats_ref[0], f32))
        decay_log = rate * (
            jnp.maximum(decay_raw, 0.0) + jnp.log1p(jnp.exp(-jnp.abs(decay_raw)))
        )
        row, col = iota((128, 128), 0), iota((128, 128), 1)
        upto = jnp.where(row <= col, 1.0, 0.0)
        eye = jnp.where(row == col, 1.0, 0.0)
        cumulative = exact(decay_log, upto, 1, 0)
        beta = jax.nn.sigmoid(beta_raw)
        gate_ref[0] = cumulative
        gate_ref[1] = beta
        gate_ref[2] = rate * jax.nn.sigmoid(decay_raw)
        padding = jnp.zeros((112, 128), f32)
        column_ref[0] = exact(eye, jnp.concatenate([cumulative, padding], 0), 1, 1)
        column_ref[1] = exact(eye, jnp.concatenate([beta, padding], 0), 1, 1)
        carry_ref[...] = jnp.concatenate([jnp.zeros((DK, DV), f32), eye], 1)

    for local in range(STEP_BLOCKS):
        block = here * STEP_BLOCKS + local
        weighted, entry, last, row, col = block_gates(block, ints_ref, gate_ref, column_ref)
        _, _, _, _, query, keys = normed(x_ref, local)
        values = block_rows(x_ref, local, 2)
        grads = block_rows(x_ref, local, 3)
        both = mm_nt(jnp.concatenate([keys, query], 0), keys)
        strict = jnp.where(row > col, weighted * both[:GROUP], 0.0)
        inverse = triangular_inverse(strict, row, col).astype(bf16)
        mixing = (weighted * both[GROUP:]).astype(bf16)
        keys_entry = (keys.astype(f32) * entry).astype(bf16)
        keys_last = (keys.astype(f32) * last).astype(bf16)
        first = mm(inverse, jnp.concatenate([values, keys_entry], 1))
        fresh, seen = first[:, :DV], first[:, DV:].astype(bf16)
        pair = jnp.concatenate([fresh.astype(bf16), seen], 1)
        mixed = mm(mixing, pair)
        read = (entry * query.astype(f32) - mixed[:, DV:]).astype(bf16)
        written = mm_tn(keys_last, pair)
        back = mm_tn(mixing, grads)
        pushed = mm_tn(inverse, jnp.concatenate([back.astype(bf16), keys_last], 1))
        step = written[:, DV:].astype(bf16)
        fresh_ref[local] = fresh
        out_ref[local] = mixed[:, :DV]
        push_ref[local] = pushed[:, :DV]
        maps_ref[local, 0] = seen
        maps_ref[local, 1] = read
        maps_ref[local, 2] = pushed[:, DV:].astype(bf16)
        step_ref[block] = step
        term_ref[block] = mm_tn(read, grads)
        carried = carry_ref[...]
        prefix_free_ref[local] = carried[:, :DV]
        prefix_ref[local] = carried[:, DV:].astype(bf16)
        last_entry = entry[GROUP - 1 :, :]
        moved = last_entry * carried - mm(step, carried)
        carry_ref[...] = moved + jnp.concatenate(
            [written[:, :DV], jnp.zeros((DK, DK), f32)], 1
        )
        term_ref[16 + block] = jnp.broadcast_to(last_entry, (DK, DV))

    @pl.when(here == pl.num_programs(0) - 1)
    def epilogue():
        row, col = iota((128, 128), 0), iota((128, 128), 1)
        eye = jnp.where(row == col, 1.0, 0.0)
        adjoint = jnp.concatenate([jnp.zeros((DK, DV), f32), eye], 1)
        for block in range(15, -1, -1):
            suffix_free_ref[block] = adjoint[:, :DV]
            suffix_ref[block] = adjoint[:, DV:].astype(bf16)
            scale = jnp.concatenate([term_ref[16 + block]] * 2, 1)
            moved = scale * adjoint - mm_tn(step_ref[block], adjoint)
            adjoint = moved + jnp.concatenate([term_ref[block], jnp.zeros((DK, DK), f32)], 1)
        free = carry_ref[:, :DV].astype(bf16)
        total = carry_ref[:, DV:].astype(bf16)
        term = adjoint[:, :DV].astype(bf16)
        for other in range(8):
            send_ref[other, :DK] = total
            send_ref[other, DK:] = jnp.where(ints_ref[0] < other, free, term)


def tables(ints, floats, received):
    blocks = received.shape[0] // 2
    steps = blocks // STEP_BLOCKS
    wide = jax.ShapeDtypeStruct((blocks, GROUP, DV), f32)
    half = jax.ShapeDtypeStruct((blocks, DK, DV), bf16)
    by_step = pl.BlockSpec((STEP_BLOCKS, GROUP, DV), lambda i: (i, 0, 0))
    whole = lambda *shape: pl.BlockSpec(shape, lambda i: (0,) * len(shape))
    return pl.pallas_call(
        tables_kernel,
        grid=(steps,),
        in_specs=[
            pl.BlockSpec(memory_space=pltpu.SMEM),
            pl.BlockSpec(memory_space=pltpu.SMEM),
            pl.BlockSpec((2 * blocks, GATE_ROWS, 128), lambda i: (0, 256 // GATE_ROWS, 0)),
            pl.BlockSpec((2 * STEP_BLOCKS, 256 + GATE_ROWS, 128), lambda i: (i, 0, 0)),
        ],
        out_specs=[
            whole(8, 256, 128),
            whole(3, blocks, 128),
            whole(2, 128, 128),
            by_step,
            by_step,
            by_step,
            pl.BlockSpec((STEP_BLOCKS, 3, GROUP, DV), lambda i: (i, 0, 0, 0)),
            by_step,
            by_step,
            whole(blocks, DK, DV),
            whole(blocks, DK, DV),
        ],
        out_shape=[
            jax.ShapeDtypeStruct((8, 256, 128), bf16),
            jax.ShapeDtypeStruct((3, blocks, 128), f32),
            jax.ShapeDtypeStruct((2, 128, 128), f32),
            wide,
            wide,
            wide,
            jax.ShapeDtypeStruct((blocks, 3, GROUP, DV), bf16),
            half,
            wide,
            half,
            wide,
        ],
        scratch_shapes=[
            pltpu.VMEM((blocks, DK, DK), bf16),
            pltpu.VMEM((2 * blocks, DK, DV), f32),
            pltpu.VMEM((DK, DV + DK), f32),
        ],
        compiler_params=pltpu.CompilerParams(
            dimension_semantics=("arbitrary",), vmem_limit_bytes=VMEM_BYTES
        ),
        name="tables",
    )(ints, floats, received, received)


def split_two(state):
    high = state.astype(bf16)
    return jnp.concatenate([high, (state - high.astype(f32)).astype(bf16)], 1)


def gradients_kernel(
    ints_ref,
    x_ref,
    shards_ref,
    gate_ref,
    column_ref,
    fresh_ref,
    out_ref,
    push_ref,
    maps_ref,
    prefix_ref,
    prefix_free_ref,
    suffix_ref,
    suffix_free_ref,
    y_ref,
    ends_ref,
):
    here = pl.program_id(0)

    @pl.when(here == 0)
    def prologue():
        me = ints_ref[0]
        state = jnp.zeros((DK, DV), f32)
        adjoint = jnp.zeros((DK, DV), f32)
        for k in range(7):
            moved = mm(shards_ref[k, :DK], split_two(state))
            new = moved[:, :DV] + moved[:, DV:] + shards_ref[k, DK:].astype(f32)
            state = jnp.where(k < me, new, state)
            at = 7 - k
            moved = mm_tn(shards_ref[at, :DK], split_two(adjoint))
            new = moved[:, :DV] + moved[:, DV:] + shards_ref[at, DK:].astype(f32)
            adjoint = jnp.where(at > me, new, adjoint)
        ends_ref[0] = state.astype(bf16)
        ends_ref[1] = adjoint.astype(bf16)

    lane = iota((GROUP, 8), 1)
    sublane = iota((8, GROUP), 0)
    change_cols = jnp.zeros((GROUP, 8), f32)
    beta_cols = jnp.zeros((GROUP, 8), f32)
    column_sums = jnp.zeros((8, GROUP), f32)
    for local in range(STEP_BLOCKS):
        block = here * STEP_BLOCKS + local
        weighted, entry, last, row, col = block_gates(block, ints_ref, gate_ref, column_ref)
        query_raw, key_raw, query_root, key_root, query, keys = normed(x_ref, local)
        grads = block_rows(x_ref, local, 3)
        state = prefix_free_ref[local] + mm(prefix_ref[local], ends_ref[0])
        adjoint = suffix_free_ref[local] + mm(suffix_ref[local], ends_ref[1])
        state_low, adjoint_low = state.astype(bf16), adjoint.astype(bf16)
        read = mm(maps_ref[local, 0:2].reshape(2 * GROUP, DK), state_low)
        fresh = (fresh_ref[local] - read[:GROUP]).astype(bf16)
        outputs = out_ref[local] + read[GROUP:]
        pushed = push_ref[local] + mm(maps_ref[local, 2], adjoint_low)
        sides = jnp.concatenate([grads, pushed.astype(bf16)], 0)
        on_fresh = mm_nt(sides, fresh)
        on_state = mm_nt(sides, state_low)
        on_adjoint = mm_nt(fresh, adjoint_low)
        both = mm_nt(jnp.concatenate([keys, query], 0), keys)
        mix_term = weighted * on_fresh[:GROUP]
        key_term = jnp.where(row > col, -weighted * on_fresh[GROUP:], 0.0)
        query_entry = entry * on_state[:GROUP]
        key_entry = -entry * on_state[GROUP:]
        key_last = last * on_adjoint
        stacked = jnp.concatenate([mix_term.astype(bf16), key_term.astype(bf16)], 0)
        direct = mm(stacked, keys)
        turned = mm_tn(stacked, jnp.concatenate([query, keys], 0))
        query_grad = query_entry + direct[:GROUP]
        key_grad = key_entry + key_last + direct[GROUP:] + turned
        query_wide, key_wide = query.astype(f32), keys.astype(f32)
        table = mix_term * both[GROUP:] + key_term * both[:GROUP]
        last_sums = jnp.sum(key_wide * key_last, axis=1, keepdims=True)
        change = (
            jnp.sum(table + query_wide * query_entry + key_wide * key_entry, axis=1, keepdims=True)
            - last_sums
        )
        extra = jnp.sum(last_sums, axis=0, keepdims=True) + entry[GROUP - 1 :, :] * jnp.sum(
            jnp.sum(adjoint * state, axis=1, keepdims=True), axis=0, keepdims=True
        )
        change = change + jnp.where(iota((GROUP, 1), 0) == GROUP - 1, extra, 0.0)
        change_cols = jnp.where(lane == local, change, change_cols)
        beta_cols = jnp.where(lane == local, last_sums, beta_cols)
        column_sums = jnp.where(
            sublane == local, jnp.sum(table, axis=0, keepdims=True), column_sums
        )
        query_grad = query_grad * DK ** (-0.5)
        query_dot = jnp.sum(query_grad * query_raw, axis=1, keepdims=True)
        key_dot = jnp.sum(key_grad * key_raw, axis=1, keepdims=True)
        query_back = query_root * query_grad - query_raw * (
            query_root * query_root * query_root * query_dot
        )
        key_back = key_root * key_grad - key_raw * (key_root * key_root * key_root * key_dot)
        for half in range(2):
            rows = slice(64 * half, 64 * half + 64)
            at = 2 * local + half
            y_ref[at, 0:64, :] = outputs[rows].astype(bf16)
            y_ref[at, 64:128, :] = query_back[rows].astype(bf16)
            y_ref[at, 128:192, :] = key_back[rows].astype(bf16)
            y_ref[at, 192:256, :] = pushed[rows].astype(bf16)

    row, col = iota((GROUP, GROUP), 0), iota((GROUP, GROUP), 1)
    after = jnp.where(row >= col, 1.0, 0.0)
    eye = jnp.where(row == col, 1.0, 0.0)
    decay_rows = exact(change_cols, after, 0, 0) - exact(column_sums, after, 1, 0)
    beta_rows = exact(beta_cols, eye, 0, 0) + column_sums
    for local in range(STEP_BLOCKS):
        block = here * STEP_BLOCKS + local
        decay_grad = decay_rows[local : local + 1] * gate_ref[2, pl.ds(block, 1), :]
        beta_grad = beta_rows[local : local + 1] * (1.0 - gate_ref[1, pl.ds(block, 1), :])
        rows = iota((GATE_ROWS, 128), 0)
        tail = jnp.where(rows == 0, decay_grad, jnp.where(rows == 1, beta_grad, 0.0)).astype(bf16)
        for half in range(2):
            y_ref[2 * local + half, 256:, :] = tail


def gradients(ints, received, shards, *made):
    blocks = received.shape[0] // 2
    steps = blocks // STEP_BLOCKS
    by_step = pl.BlockSpec((STEP_BLOCKS, GROUP, DV), lambda i: (i, 0, 0))
    whole = lambda *shape: pl.BlockSpec(shape, lambda i: (0,) * len(shape))
    rows_spec = pl.BlockSpec((2 * STEP_BLOCKS, 256 + GATE_ROWS, 128), lambda i: (i, 0, 0))
    return pl.pallas_call(
        gradients_kernel,
        grid=(steps,),
        in_specs=[
            pl.BlockSpec(memory_space=pltpu.SMEM),
            rows_spec,
            whole(8, 256, 128),
            whole(3, blocks, 128),
            whole(2, 128, 128),
            by_step,
            by_step,
            by_step,
            pl.BlockSpec((STEP_BLOCKS, 3, GROUP, DV), lambda i: (i, 0, 0, 0)),
            by_step,
            by_step,
            by_step,
            by_step,
        ],
        out_specs=rows_spec,
        out_shape=jax.ShapeDtypeStruct(received.shape, bf16),
        scratch_shapes=[pltpu.VMEM((2, DK, DV), bf16)],
        compiler_params=pltpu.CompilerParams(
            dimension_semantics=("arbitrary",), vmem_limit_bytes=VMEM_BYTES
        ),
        name="gradients",
    )(ints, received, shards, *made)


def pack_kernel(query_ref, key_ref, value_ref, decay_ref, beta_ref, grad_ref, x_ref):
    row, col = iota((64, 128), 0), iota((64, 128), 1)
    twice = jnp.where((col == row) | (col == row + 64), 1.0, 0.0).astype(bf16)
    decay = mm_tn(decay_ref[...], twice)
    beta = mm_tn(beta_ref[...], twice)
    rows = iota((GATE_ROWS, 128), 0)
    for head in range(VALUE_HEAD_COUNT):
        shared = slice(DK * (head // 2), DK * (head // 2) + DK)
        own = slice(DV * head, DV * head + DV)
        x_ref[head, 0:64, :] = query_ref[:, shared]
        x_ref[head, 64:128, :] = key_ref[:, shared]
        x_ref[head, 128:192, :] = value_ref[:, own]
        x_ref[head, 192:256, :] = grad_ref[:, own]
        x_ref[head, 256:, :] = jnp.where(
            rows == 0,
            decay[head : head + 1],
            jnp.where(rows == 1, beta[head : head + 1], 0.0),
        ).astype(bf16)


def pack(query, key, value, decay, beta, grad):
    return pl.pallas_call(
        pack_kernel,
        out_shape=jax.ShapeDtypeStruct((VALUE_HEAD_COUNT, 256 + GATE_ROWS, 128), bf16),
        compiler_params=pltpu.CompilerParams(vmem_limit_bytes=VMEM_BYTES),
        name="pack",
    )(query, key, value, decay, beta, grad)


def unpack_kernel(ints_ref, y_ref, out_ref, query_ref, key_ref, value_ref, decay_ref, beta_ref):
    row, col = iota((128, 64), 0), iota((128, 64), 1)
    select = jnp.where(row == col + 64 * ints_ref[5], 1.0, 0.0).astype(bf16)
    for head in range(VALUE_HEAD_COUNT):
        own = slice(DV * head, DV * head + DV)
        out_ref[:, own] = y_ref[head, 0:64, :]
        value_ref[:, own] = y_ref[head, 192:256, :]
    for head in range(NK):
        shared = slice(DK * head, DK * head + DK)
        for part, ref in ((1, query_ref), (2, key_ref)):
            rows = slice(64 * part, 64 * part + 64)
            summed = y_ref[2 * head, rows, :].astype(f32) + y_ref[2 * head + 1, rows, :].astype(f32)
            ref[:, shared] = summed.astype(bf16)
    tail = y_ref[:, 256:, :].astype(f32)
    rows = iota(tail.shape, 1)
    for index, ref in ((0, decay_ref), (1, beta_ref)):
        picked = jnp.sum(jnp.where(rows == index, tail, 0.0), axis=1)
        ref[...] = contract(select, picked, 0, 1).astype(bf16)


def unpack(ints, returned):
    wide = jax.ShapeDtypeStruct((64, VALUE_HEAD_COUNT * DV), bf16)
    narrow = jax.ShapeDtypeStruct((64, NK * DK), bf16)
    gates = jax.ShapeDtypeStruct((64, VALUE_HEAD_COUNT), bf16)
    vmem = pl.BlockSpec(memory_space=pltpu.VMEM)
    return pl.pallas_call(
        unpack_kernel,
        in_specs=[pl.BlockSpec(memory_space=pltpu.SMEM), vmem],
        out_specs=[vmem] * 6,
        out_shape=[wide, narrow, narrow, wide, gates, gates],
        compiler_params=pltpu.CompilerParams(vmem_limit_bytes=VMEM_BYTES),
        name="unpack",
    )(ints, returned)


def local(
    query_raw,
    key_raw,
    value_raw,
    decay_raw,
    beta_raw,
    decay_base,
    decay_bias,
    doc_lengths,
    out_grad,
):
    head = lax.axis_index("head")
    shard = lax.axis_index("ctx")
    sent = pack(query_raw, key_raw, value_raw, decay_raw, beta_raw, out_grad)
    received = lax.all_to_all(sent, "head", split_axis=0, concat_axis=0, tiled=True)
    ends = [jnp.sum(doc_lengths[:j]) for j in range(4)]
    ints = jnp.stack([shard.astype(jnp.int32), *ends, (head % 2).astype(jnp.int32)])
    floats = jnp.stack(
        [
            lax.dynamic_index_in_dim(decay_base, head, keepdims=False),
            lax.dynamic_index_in_dim(decay_bias, head, keepdims=False),
        ]
    )
    send, *made = tables(ints, floats, received)
    shards = lax.all_to_all(send, "ctx", split_axis=0, concat_axis=0, tiled=True)
    back = gradients(ints, received, shards, *made)
    returned = lax.all_to_all(back, "head", split_axis=0, concat_axis=0, tiled=True)
    output, query_grad, key_grad, value_grad, decay_grad, beta_grad = unpack(ints, returned)
    return (output, query_grad, key_grad, value_grad, decay_grad, beta_grad)


def solution(mesh):
    placed = (
        P(("ctx", "head"), None),
        P(("ctx", "head"), None),
        P(("ctx", "head"), None),
        P(("ctx", "head"), None),
        P(("ctx", "head"), None),
        P(),
        P(),
        P(),
        P(("ctx", "head"), None),
    )
    return jax.shard_map(
        local,
        mesh=mesh,
        in_specs=placed,
        out_specs=(P(("ctx", "head"), None),) * 6,
        check_vma=False,
    )
```

```python
import functools

import jax
import jax.numpy as jnp
from jax import lax
from jax.experimental import pallas as pl
from jax.experimental.pallas import tpu as pltpu
from jax.sharding import PartitionSpec as P

VALUE_HEAD_COUNT = 32
NK = 16
DK = 128
DV = 128
GROUP = 128
GATE_ROWS = 16
PACK_HEADS = 16
STATE_BLOCKS = 8
OUTPUT_BLOCKS = 8
GRADIENT_BLOCKS = 4
BLOCKS = 16
SHARDS = 8
VMEM_BYTES = 60 * 1024 * 1024

bf16 = jnp.bfloat16
f32 = jnp.float32


def contract(left, right, left_dim, right_dim):
    return lax.dot_general(
        left.astype(bf16),
        right.astype(bf16),
        (((left_dim,), (right_dim,)), ((), ())),
        preferred_element_type=f32,
    )


def mm(left, right):
    return contract(left, right, 1, 0)


def mm_nt(left, right):
    return contract(left, right, 1, 1)


def mm_tn(left, right):
    return contract(left, right, 0, 0)


def exact(left, right, left_dim, right_dim):
    return lax.dot_general(
        left,
        right,
        (((left_dim,), (right_dim,)), ((), ())),
        preferred_element_type=f32,
        precision=lax.Precision.HIGHEST,
    )


def iota(shape, dim):
    return lax.broadcasted_iota(jnp.int32, shape, dim)


def segment_of(positions, starts):
    count = jnp.zeros(positions.shape, jnp.int32)
    for start in starts:
        count = count + jnp.where(positions >= start, 1, 0)
    return count


def pick_column(table, block):
    lane = iota(table.shape, 1)
    return jnp.sum(jnp.where(lane == block, table, 0.0), axis=1, keepdims=True)


def block_gates(block, ints_ref, gate_ref, column_ref):
    starts = [ints_ref[1 + j] for j in range(4)]
    first = ints_ref[0] * 16 * GROUP + block * GROUP
    cum_row = gate_ref[0, pl.ds(block, 1), :]
    beta_row = gate_ref[1, pl.ds(block, 1), :]
    cum_col = pick_column(column_ref[0], block)
    beta_col = pick_column(column_ref[1], block)
    seg_row = segment_of(first + iota((1, GROUP), 1), starts)
    seg_col = segment_of(first + iota((GROUP, 1), 0), starts)
    before = segment_of(jnp.full((1, 1), first - 1, jnp.int32), starts)
    row, col = iota((GROUP, GROUP), 0), iota((GROUP, GROUP), 1)
    joined = (row >= col) & (seg_col == seg_row)
    spread = jnp.where(joined, cum_col - cum_row, 0.0)
    weighted = jnp.where(joined, jnp.exp(spread), 0.0) * beta_row
    entry = jnp.where(seg_col == before, jnp.exp(cum_col), 0.0)
    cum_last = cum_col[GROUP - 1 :, :]
    same_last = seg_col == seg_col[GROUP - 1 :, :]
    last = (
        jnp.where(same_last, jnp.exp(jnp.where(same_last, cum_last - cum_col, 0.0)), 0.0) * beta_col
    )
    return weighted, entry, last


def inverse_root(raw):
    return lax.rsqrt(jnp.sum(raw * raw, axis=1, keepdims=True) + 1e-06)


def block_rows(ref, block, part):
    return jnp.concatenate(
        [ref[2 * block + half, 64 * part : 64 * part + 64, :] for half in range(2)], axis=0
    )


def eye_of(size):
    return jnp.where(iota((size, size), 0) == iota((size, size), 1), 1.0, 0.0)


def split_rows(matrix):
    high = matrix.astype(bf16)
    return jnp.concatenate([high, (matrix - high.astype(f32)).astype(bf16)], 0)


def cost(units):
    return pl.CostEstimate(
        flops=units * BLOCKS * 2 * 128**3 * 8, bytes_accessed=1 << 20, transcendentals=0
    )


def triangular_inverses(stricts, row, col):
    differ = row ^ col
    eye = jnp.where(differ == 0, 1.0, 0.0)
    inverses = [eye - jnp.where(differ == 1, strict, 0.0) for strict in stricts]
    for level in range(1, 7):
        size = 1 << level
        band = (differ >= size) & (differ < 2 * size)
        held = [inverse.astype(bf16) for inverse in inverses]
        half = [
            mm(one, jnp.where(band, strict, 0.0)) for one, strict in zip(held, stricts)
        ]
        step = [mm(one, other) for one, other in zip(half, held)]
        inverses = [inverse - one for inverse, one in zip(inverses, step)]
    held = [inverse.astype(bf16) for inverse in inverses]
    upper = [strict.astype(bf16) for strict in stricts]
    lower = [(strict - one.astype(f32)).astype(bf16) for strict, one in zip(stricts, upper)]
    rest = [mm(one, other) for one, other in zip(upper, held)]
    fine = [mm(one, other) for one, other in zip(lower, held)]
    rest = [
        eye - one.astype(f32) - high - low for one, high, low in zip(held, rest, fine)
    ]
    return [one.astype(f32) + mm(one, other) for one, other in zip(held, rest)]


def maps_kernel(
    ints_ref,
    floats_ref,
    x_ref,
    gate_ref,
    column_ref,
    keys_ref,
    inverse_ref,
    seen_ref,
    back_ref,
    step_ref,
    prefix_ref,
    suffix_ref,
    total_ref,
):
    tail = x_ref[:, 64:, :].astype(f32)
    paired = tail.reshape(BLOCKS, 2, GATE_ROWS, 128)
    lane = iota((BLOCKS, GATE_ROWS, 128), 2)
    rows = iota((BLOCKS, GATE_ROWS, 128), 1)
    tail = jnp.where(lane < 64, paired[:, 0], paired[:, 1])
    decay_raw = jnp.sum(jnp.where(rows == 0, tail, 0.0), axis=1) + floats_ref[1]
    beta_raw = jnp.sum(jnp.where(rows == 1, tail, 0.0), axis=1)
    rate = -jnp.exp(jnp.full((BLOCKS, 128), floats_ref[0], f32))
    decay_log = rate * (jnp.maximum(decay_raw, 0.0) + jnp.log1p(jnp.exp(-jnp.abs(decay_raw))))
    row, col = iota((128, 128), 0), iota((128, 128), 1)
    eye = eye_of(128)
    cumulative = exact(decay_log, jnp.where(row <= col, 1.0, 0.0), 1, 0)
    beta = jax.nn.sigmoid(beta_raw)
    gate_ref[0] = cumulative
    gate_ref[1] = beta
    gate_ref[2] = rate * jax.nn.sigmoid(decay_raw)
    padding = jnp.zeros((128 - BLOCKS, 128), f32)
    column_ref[0] = exact(eye, jnp.concatenate([cumulative, padding], 0), 1, 1)
    column_ref[1] = exact(eye, jnp.concatenate([beta, padding], 0), 1, 1)

    each = range(BLOCKS)
    gates = [block_gates(i, ints_ref, gate_ref, column_ref) for i in each]
    raws = [block_rows(x_ref, i, 0).astype(f32) for i in each]
    keys = [(raw * inverse_root(raw)).astype(bf16) for raw in raws]
    both = [mm_nt(one, one) for one in keys]
    stricts = [jnp.where(row > col, gates[i][0] * both[i], 0.0) for i in each]
    inverses = [one.astype(bf16) for one in triangular_inverses(stricts, row, col)]
    keys_entry = [(keys[i].astype(f32) * gates[i][1]).astype(bf16) for i in each]
    keys_last = [(keys[i].astype(f32) * gates[i][2]).astype(bf16) for i in each]
    seen = [mm(inverses[i], keys_entry[i]).astype(bf16) for i in each]
    back = [mm_tn(inverses[i], keys_last[i]).astype(bf16) for i in each]
    steps = [mm_tn(keys_last[i], seen[i]).astype(bf16) for i in each]
    scales = [gates[i][1][GROUP - 1 :, :] for i in each]
    for i in each:
        keys_ref[i] = keys[i]
        inverse_ref[i] = inverses[i]
        seen_ref[i] = seen[i]
        back_ref[i] = back[i]
        step_ref[i] = steps[i]
        gate_ref[3, i : i + 1, :] = jnp.broadcast_to(scales[i], (1, 128))
    forward, backward = eye, eye
    for i in each:
        other = BLOCKS - 1 - i
        forward_low, backward_low = forward.astype(bf16), backward.astype(bf16)
        prefix_ref[i] = forward_low
        suffix_ref[other] = backward_low
        forward = scales[i] * forward - mm(steps[i], forward_low)
        backward = scales[other] * backward - mm_tn(steps[other], backward_low)
    total_ref[...] = forward.astype(bf16)


def maps(ints, floats, keys_got):
    half = jax.ShapeDtypeStruct((BLOCKS, GROUP, DK), bf16)
    vmem = pl.BlockSpec(memory_space=pltpu.VMEM)
    smem = pl.BlockSpec(memory_space=pltpu.SMEM)
    return pl.pallas_call(
        maps_kernel,
        in_specs=[smem, smem, vmem],
        out_specs=[vmem] * 10,
        out_shape=[
            jax.ShapeDtypeStruct((4, BLOCKS, 128), f32),
            jax.ShapeDtypeStruct((2, 128, 128), f32),
            *[half] * 7,
            jax.ShapeDtypeStruct((DK, DK), bf16),
        ],
        compiler_params=pltpu.CompilerParams(vmem_limit_bytes=VMEM_BYTES),
        cost_estimate=cost(20),
        name="maps",
    )(ints, floats, keys_got)


def compose_kernel(ints_ref, *refs):
    total_refs, (forward_ref, backward_ref) = refs[: SHARDS - 1], refs[SHARDS - 1 :]
    me = ints_ref[0]
    forward, backward = eye_of(DK), eye_of(DK)
    for k in range(1, SHARDS):
        at = slice(DK * (k - 1), DK * k)
        forward_ref[:, at] = jnp.where(k <= me, forward, 0.0).astype(bf16)
        backward_ref[:, at] = jnp.where(me + k < SHARDS, backward, 0.0).astype(bf16)
        if k < SHARDS - 1:
            moved = mm(split_rows(forward), total_refs[k - 1][...])
            forward = moved[:DK] + moved[DK:]
            moved = mm_nt(split_rows(backward), total_refs[SHARDS - 1 - k][...])
            backward = moved[:DK] + moved[DK:]


def compose(ints, totals):
    vmem = pl.BlockSpec(memory_space=pltpu.VMEM)
    smem = pl.BlockSpec(memory_space=pltpu.SMEM)
    wide = jax.ShapeDtypeStruct((DK, (SHARDS - 1) * DK), bf16)
    return pl.pallas_call(
        compose_kernel,
        in_specs=[smem] + [vmem] * (SHARDS - 1),
        out_specs=[vmem] * 2,
        out_shape=[wide, wide],
        compiler_params=pltpu.CompilerParams(vmem_limit_bytes=VMEM_BYTES),
        cost_estimate=cost(2),
        name="compose",
    )(ints, *totals)


def states_kernel(
    ints_ref,
    x_ref,
    gate_ref,
    column_ref,
    keys_ref,
    inverse_ref,
    seen_ref,
    step_ref,
    fresh_ref,
    out_ref,
    push_ref,
    read_ref,
    prefix_ref,
    suffix_ref,
    *rest,
):
    send_refs, (term_ref, carry_ref) = rest[: SHARDS - 1], rest[SHARDS - 1 :]
    here = pl.program_id(0)

    @pl.when(here == 0)
    def prologue():
        carry_ref[...] = jnp.zeros((DK, DV), f32)

    each = range(STATE_BLOCKS)
    first = here * STATE_BLOCKS
    gates = [block_gates(first + i, ints_ref, gate_ref, column_ref) for i in each]
    raws = [block_rows(x_ref, i, 0).astype(f32) for i in each]
    queries = [(raw * inverse_root(raw) * DK ** (-0.5)).astype(bf16) for raw in raws]
    keys = [keys_ref[i] for i in each]
    grads = [block_rows(x_ref, i, 2) for i in each]
    mixing = [(gates[i][0] * mm_nt(queries[i], keys[i])).astype(bf16) for i in each]
    fresh = [mm(inverse_ref[i], block_rows(x_ref, i, 1)) for i in each]
    back = [mm_tn(mixing[i], grads[i]).astype(bf16) for i in each]
    pairs = [jnp.concatenate([fresh[i].astype(bf16), seen_ref[i]], 1) for i in each]
    mixed = [mm(mixing[i], pairs[i]) for i in each]
    keys_last = [(keys[i].astype(f32) * gates[i][2]).astype(bf16) for i in each]
    written = [mm_tn(keys_last[i], pairs[i][:, :DV]) for i in each]
    reads = [(gates[i][1] * queries[i].astype(f32) - mixed[i][:, DV:]).astype(bf16) for i in each]
    terms = [mm_tn(reads[i], grads[i]) for i in each]
    pushed = [mm_tn(inverse_ref[i], back[i]) for i in each]
    carried = carry_ref[...]
    for i in each:
        block = first + i
        fresh_ref[i] = pairs[i][:, :DV]
        out_ref[i] = mixed[i][:, :DV].astype(bf16)
        push_ref[i] = pushed[i].astype(bf16)
        read_ref[i] = reads[i]
        term_ref[block] = terms[i]
        carried_low = carried.astype(bf16)
        prefix_ref[i] = carried_low
        carried = (
            gate_ref[3, pl.ds(block, 1), :] * carried
            - mm(step_ref[block], carried_low)
            + written[i]
        )
    carry_ref[...] = carried

    @pl.when(here == pl.num_programs(0) - 1)
    def epilogue():
        adjoint = jnp.zeros((DK, DV), f32)
        for block in range(BLOCKS - 1, -1, -1):
            adjoint_low = adjoint.astype(bf16)
            suffix_ref[block] = adjoint_low
            adjoint = (
                gate_ref[3, block : block + 1, :] * adjoint
                - mm_tn(step_ref[block], adjoint_low)
                + term_ref[block]
            )
        for k, ref in enumerate(send_refs):
            ref[...] = jnp.where(
                ints_ref[0] + k + 1 < SHARDS, carry_ref[...], adjoint
            ).astype(bf16)


def whole(*shape):
    return pl.BlockSpec(shape, lambda i: (0,) * len(shape))


def stepped(count, *shape):
    return pl.BlockSpec((count, *shape), lambda i: (i,) + (0,) * len(shape))


def states(ints, others, gate, column, keys, inverse, seen, step):
    half = jax.ShapeDtypeStruct((BLOCKS, GROUP, DK), bf16)
    by_step = stepped(STATE_BLOCKS, GROUP, DK)
    square = jax.ShapeDtypeStruct((DK, DV), bf16)
    return pl.pallas_call(
        states_kernel,
        grid=(BLOCKS // STATE_BLOCKS,),
        in_specs=[
            pl.BlockSpec(memory_space=pltpu.SMEM),
            stepped(2 * STATE_BLOCKS, 192, 128),
            whole(4, BLOCKS, 128),
            whole(2, 128, 128),
            by_step,
            by_step,
            by_step,
            whole(BLOCKS, DK, DK),
        ],
        out_specs=[by_step] * 5 + [whole(BLOCKS, DK, DV)] + [whole(DK, DV)] * (SHARDS - 1),
        out_shape=[half] * 6 + [square] * (SHARDS - 1),
        scratch_shapes=[pltpu.VMEM((BLOCKS, DK, DV), f32), pltpu.VMEM((DK, DV), f32)],
        compiler_params=pltpu.CompilerParams(
            dimension_semantics=("arbitrary",), vmem_limit_bytes=VMEM_BYTES
        ),
        cost_estimate=cost(14),
        name="states",
    )(ints, others, gate, column, keys, inverse, seen, step)


def outputs_kernel(
    forward_ref,
    backward_ref,
    seen_ref,
    back_ref,
    prefix_map_ref,
    suffix_map_ref,
    fresh_ref,
    out_ref,
    push_ref,
    read_ref,
    prefix_ref,
    suffix_ref,
    *rest,
):
    end_refs, (y_ref, state_ref, adjoint_ref, made_ref, ends_ref) = (
        rest[: SHARDS - 1],
        rest[SHARDS - 1 :],
    )

    @pl.when(pl.program_id(0) == 0)
    def prologue():
        got = [ref[...] for ref in end_refs]
        ends_ref[0] = mm(forward_ref[...], jnp.concatenate(got, 0)).astype(bf16)
        ends_ref[1] = mm(backward_ref[...], jnp.concatenate(got[::-1], 0)).astype(bf16)

    each = range(OUTPUT_BLOCKS)
    state_end, adjoint_end = ends_ref[0], ends_ref[1]
    low = [
        (prefix_ref[i].astype(f32) + mm(prefix_map_ref[i], state_end)).astype(bf16) for i in each
    ]
    adjoints = [
        (suffix_ref[i].astype(f32) + mm(suffix_map_ref[i], adjoint_end)).astype(bf16) for i in each
    ]
    fresh = [fresh_ref[i].astype(f32) - mm(seen_ref[i], low[i]) for i in each]
    outputs = [out_ref[i].astype(f32) + mm(read_ref[i], low[i]) for i in each]
    pushed = [push_ref[i].astype(f32) + mm(back_ref[i], adjoints[i]) for i in each]
    for i in each:
        state_ref[i] = low[i]
        adjoint_ref[i] = adjoints[i]
        made_ref[i] = fresh[i].astype(bf16)
        for half in range(2):
            rows = slice(64 * half, 64 * half + 64)
            y_ref[2 * i + half, :64, :] = outputs[i][rows].astype(bf16)
            y_ref[2 * i + half, 64:, :] = pushed[i][rows].astype(bf16)


def outputs(forward, backward, blocks, ends):
    half = jax.ShapeDtypeStruct((BLOCKS, GROUP, DK), bf16)
    by_step = stepped(OUTPUT_BLOCKS, GROUP, DK)
    return pl.pallas_call(
        outputs_kernel,
        grid=(BLOCKS // OUTPUT_BLOCKS,),
        in_specs=[whole(DK, (SHARDS - 1) * DK)] * 2
        + [by_step] * 10
        + [whole(DK, DV)] * (SHARDS - 1),
        out_specs=[stepped(2 * OUTPUT_BLOCKS, 128, 128)] + [by_step] * 3,
        out_shape=[jax.ShapeDtypeStruct((2 * BLOCKS, 128, 128), bf16)] + [half] * 3,
        scratch_shapes=[pltpu.VMEM((2, DK, DV), bf16)],
        compiler_params=pltpu.CompilerParams(
            dimension_semantics=("arbitrary",), vmem_limit_bytes=VMEM_BYTES
        ),
        cost_estimate=cost(5),
        name="outputs",
    )(forward, backward, *blocks, *ends)


def gradients_kernel(
    ints_ref,
    keys_got_ref,
    others_ref,
    gate_ref,
    column_ref,
    keys_ref,
    y_ref,
    state_ref,
    adjoint_ref,
    made_ref,
    z_ref,
):
    here = pl.program_id(0)
    lane = iota((GROUP, 8), 1)
    sublane = iota((8, GROUP), 0)
    change_cols = jnp.zeros((GROUP, 8), f32)
    beta_cols = jnp.zeros((GROUP, 8), f32)
    column_sums = jnp.zeros((8, GROUP), f32)
    each = range(GRADIENT_BLOCKS)
    row, col = iota((GROUP, GROUP), 0), iota((GROUP, GROUP), 1)
    sides = [
        jnp.concatenate([block_rows(others_ref, i, 2), block_rows(y_ref, i, 1)], 0) for i in each
    ]
    on_fresh = [mm_nt(sides[i], made_ref[i]) for i in each]
    on_state = [mm_nt(sides[i], state_ref[i]) for i in each]
    on_adjoint = [mm_nt(made_ref[i], adjoint_ref[i]) for i in each]
    query_raws = [block_rows(others_ref, i, 0).astype(f32) for i in each]
    query_roots = [inverse_root(raw) for raw in query_raws]
    queries = [
        (query_raws[i] * query_roots[i] * DK ** (-0.5)).astype(bf16) for i in each
    ]
    keys = [keys_ref[i] for i in each]
    both = [mm_nt(jnp.concatenate([keys[i], queries[i]], 0), keys[i]) for i in each]
    gates = [
        block_gates(here * GRADIENT_BLOCKS + i, ints_ref, gate_ref, column_ref) for i in each
    ]
    mix_terms = [gates[i][0] * on_fresh[i][:GROUP] for i in each]
    key_terms = [jnp.where(row > col, -gates[i][0] * on_fresh[i][GROUP:], 0.0) for i in each]
    stacked = [
        jnp.concatenate([mix_terms[i].astype(bf16), key_terms[i].astype(bf16)], 0) for i in each
    ]
    direct = [mm(stacked[i], keys[i]) for i in each]
    turned = [mm_tn(stacked[i], jnp.concatenate([queries[i], keys[i]], 0)) for i in each]
    for i in each:
        _, entry, last = gates[i]
        query_raw, query_root = query_raws[i], query_roots[i]
        key_raw = block_rows(keys_got_ref, i, 0).astype(f32)
        key_root = inverse_root(key_raw)
        query_entry = entry * on_state[i][:GROUP]
        key_entry = -entry * on_state[i][GROUP:]
        key_last = last * on_adjoint[i]
        query_grad = query_entry + direct[i][:GROUP]
        key_grad = key_entry + key_last + direct[i][GROUP:] + turned[i]
        query_wide, key_wide = queries[i].astype(f32), keys[i].astype(f32)
        table = mix_terms[i] * both[i][GROUP:] + key_terms[i] * both[i][:GROUP]
        last_sums = jnp.sum(key_wide * key_last, axis=1, keepdims=True)
        change = (
            jnp.sum(table + query_wide * query_entry + key_wide * key_entry, axis=1, keepdims=True)
            - last_sums
        )
        overlap = adjoint_ref[i].astype(f32) * state_ref[i].astype(f32)
        extra = jnp.sum(last_sums, axis=0, keepdims=True) + entry[GROUP - 1 :, :] * jnp.sum(
            jnp.sum(overlap, axis=0, keepdims=True), axis=1, keepdims=True
        )
        change = change + jnp.where(iota((GROUP, 1), 0) == GROUP - 1, extra, 0.0)
        change_cols = jnp.where(lane == i, change, change_cols)
        beta_cols = jnp.where(lane == i, last_sums, beta_cols)
        column_sums = jnp.where(sublane == i, jnp.sum(table, axis=0, keepdims=True), column_sums)
        query_grad = query_grad * DK ** (-0.5)
        query_dot = jnp.sum(query_grad * query_raw, axis=1, keepdims=True)
        key_dot = jnp.sum(key_grad * key_raw, axis=1, keepdims=True)
        query_back = query_root * query_grad - query_raw * (
            query_root * query_root * query_root * query_dot
        )
        key_back = key_root * key_grad - key_raw * (key_root * key_root * key_root * key_dot)
        for half in range(2):
            rows = slice(64 * half, 64 * half + 64)
            z_ref[2 * i + half, 0:64, :] = query_back[rows].astype(bf16)
            z_ref[2 * i + half, 64:128, :] = key_back[rows].astype(bf16)

    after = jnp.where(row >= col, 1.0, 0.0)
    decay_rows = exact(change_cols, after, 0, 0) - exact(column_sums, after, 1, 0)
    beta_rows = exact(beta_cols, eye_of(GROUP), 0, 0) + column_sums
    for i in each:
        block = here * GRADIENT_BLOCKS + i
        decay_grad = decay_rows[i : i + 1] * gate_ref[2, pl.ds(block, 1), :]
        beta_grad = beta_rows[i : i + 1] * (1.0 - gate_ref[1, pl.ds(block, 1), :])
        rows = iota((GATE_ROWS, 128), 0)
        tail = jnp.where(rows == 0, decay_grad, jnp.where(rows == 1, beta_grad, 0.0)).astype(bf16)
        for half in range(2):
            z_ref[2 * i + half, 128:, :] = tail


def gradients(ints, keys_got, others, gate, column, keys, y, state, adjoint, made):
    by_step = stepped(GRADIENT_BLOCKS, GROUP, DK)
    rows = lambda count: stepped(2 * GRADIENT_BLOCKS, count, 128)
    return pl.pallas_call(
        gradients_kernel,
        grid=(BLOCKS // GRADIENT_BLOCKS,),
        in_specs=[
            pl.BlockSpec(memory_space=pltpu.SMEM),
            rows(64 + GATE_ROWS),
            rows(192),
            whole(4, BLOCKS, 128),
            whole(2, 128, 128),
            by_step,
            rows(128),
            by_step,
            by_step,
            by_step,
        ],
        out_specs=rows(128 + GATE_ROWS),
        out_shape=jax.ShapeDtypeStruct((2 * BLOCKS, 128 + GATE_ROWS, 128), bf16),
        compiler_params=pltpu.CompilerParams(
            dimension_semantics=("arbitrary",), vmem_limit_bytes=VMEM_BYTES
        ),
        cost_estimate=cost(14),
        name="gradients",
    )(ints, keys_got, others, gate, column, keys, y, state, adjoint, made)


def spec_wide():
    return pl.BlockSpec((64, PACK_HEADS * DV), lambda i: (0, i))


def spec_narrow():
    return pl.BlockSpec((64, PACK_HEADS * DK // 2), lambda i: (0, i))


def spec_gates():
    return pl.BlockSpec((PACK_HEADS, 64), lambda i: (i, 0))


def pack_keys_kernel(key_ref, decay_ref, beta_ref, x_ref):
    decay = jnp.concatenate([decay_ref[...].astype(f32)] * 2, 1)
    beta = jnp.concatenate([beta_ref[...].astype(f32)] * 2, 1)
    rows = iota((GATE_ROWS, 128), 0)
    for head in range(VALUE_HEAD_COUNT):
        x_ref[head, :64, :] = key_ref[:, DK * (head // 2) : DK * (head // 2) + DK]
        x_ref[head, 64:, :] = jnp.where(
            rows == 0,
            decay[head : head + 1],
            jnp.where(rows == 1, beta[head : head + 1], 0.0),
        ).astype(bf16)


def pack_keys(key, decay, beta):
    return pl.pallas_call(
        pack_keys_kernel,
        out_shape=jax.ShapeDtypeStruct((VALUE_HEAD_COUNT, 64 + GATE_ROWS, 128), bf16),
        compiler_params=pltpu.CompilerParams(vmem_limit_bytes=VMEM_BYTES),
        name="pack_keys",
    )(key, decay, beta)


def pack_others_kernel(query_ref, value_ref, grad_ref, x_ref):
    for head in range(PACK_HEADS):
        own = slice(DV * head, DV * head + DV)
        x_ref[head, 0:64, :] = query_ref[:, DK * (head // 2) : DK * (head // 2) + DK]
        x_ref[head, 64:128, :] = value_ref[:, own]
        x_ref[head, 128:192, :] = grad_ref[:, own]


def pack_others(query, value, grad):
    return pl.pallas_call(
        pack_others_kernel,
        grid=(VALUE_HEAD_COUNT // PACK_HEADS,),
        in_specs=[spec_narrow(), spec_wide(), spec_wide()],
        out_specs=stepped(PACK_HEADS, 192, 128),
        out_shape=jax.ShapeDtypeStruct((VALUE_HEAD_COUNT, 192, 128), bf16),
        compiler_params=pltpu.CompilerParams(vmem_limit_bytes=VMEM_BYTES),
        cost_estimate=cost(3),
        name="pack_others",
    )(query, value, grad)


def unpack_outputs_kernel(y_ref, out_ref, value_ref):
    for head in range(PACK_HEADS):
        own = slice(DV * head, DV * head + DV)
        out_ref[:, own] = y_ref[head, 0:64, :]
        value_ref[:, own] = y_ref[head, 64:128, :]


def unpack_outputs(returned):
    made = jax.ShapeDtypeStruct((64, VALUE_HEAD_COUNT * DV), bf16)
    return pl.pallas_call(
        unpack_outputs_kernel,
        grid=(VALUE_HEAD_COUNT // PACK_HEADS,),
        in_specs=[stepped(PACK_HEADS, 128, 128)],
        out_specs=[spec_wide()] * 2,
        out_shape=[made] * 2,
        compiler_params=pltpu.CompilerParams(vmem_limit_bytes=VMEM_BYTES),
        cost_estimate=cost(3),
        name="unpack_outputs",
    )(returned)


def unpack_gradients_kernel(ints_ref, z_ref, query_ref, key_ref, decay_ref, beta_ref):
    for head in range(PACK_HEADS // 2):
        shared = slice(DK * head, DK * head + DK)
        for part, ref in ((0, query_ref), (1, key_ref)):
            rows = slice(64 * part, 64 * part + 64)
            summed = z_ref[2 * head, rows, :].astype(f32) + z_ref[2 * head + 1, rows, :].astype(f32)
            ref[:, shared] = summed.astype(bf16)
    tail = z_ref[:, 128:, :].astype(f32)
    rows = iota(tail.shape, 1)
    for index, ref in ((0, decay_ref), (1, beta_ref)):
        picked = jnp.sum(jnp.where(rows == index, tail, 0.0), axis=1)
        ref[...] = jnp.where(ints_ref[5] == 0, picked[:, :64], picked[:, 64:]).astype(bf16)


def unpack_gradients(ints, returned):
    narrow = jax.ShapeDtypeStruct((64, NK * DK), bf16)
    gates = jax.ShapeDtypeStruct((VALUE_HEAD_COUNT, 64), bf16)
    return pl.pallas_call(
        unpack_gradients_kernel,
        grid=(VALUE_HEAD_COUNT // PACK_HEADS,),
        in_specs=[
            pl.BlockSpec(memory_space=pltpu.SMEM),
            stepped(PACK_HEADS, 128 + GATE_ROWS, 128),
        ],
        out_specs=[spec_narrow()] * 2 + [spec_gates()] * 2,
        out_shape=[narrow, narrow, gates, gates],
        compiler_params=pltpu.CompilerParams(vmem_limit_bytes=VMEM_BYTES),
        name="unpack_gradients",
    )(ints, returned)


def ring(parts, axis):
    return [
        lax.ppermute(part, axis, [(i, (i + k + 1) % SHARDS) for i in range(SHARDS)])
        for k, part in enumerate(parts)
    ]


def local(
    query_raw,
    key_raw,
    value_raw,
    decay_raw,
    beta_raw,
    decay_base,
    decay_bias,
    doc_lengths,
    out_grad,
):
    head = lax.axis_index("head")
    shard = lax.axis_index("ctx")
    ends = [jnp.sum(doc_lengths[:j]) for j in range(4)]
    ints = jnp.stack([shard.astype(jnp.int32), *ends, (head % 2).astype(jnp.int32)])
    floats = jnp.stack(
        [
            lax.dynamic_index_in_dim(decay_base, head, keepdims=False),
            lax.dynamic_index_in_dim(decay_bias, head, keepdims=False),
        ]
    )

    def to_heads(sent):
        return lax.all_to_all(sent, "head", split_axis=0, concat_axis=0, tiled=True)

    keys_got = to_heads(pack_keys(key_raw, decay_raw.T, beta_raw.T))
    others = to_heads(pack_others(query_raw, value_raw, out_grad))
    gate, column, keys, inverse, seen, back, step, prefix_map, suffix_map, total = maps(
        ints, floats, keys_got
    )
    forward, backward = compose(ints, ring([total] * (SHARDS - 1), "ctx"))
    others, forward, backward = lax.optimization_barrier((others, forward, backward))
    fresh, out, push, read, prefix, suffix, *sends = states(
        ints, others, gate, column, keys, inverse, seen, step
    )
    got = ring(sends, "ctx")
    y, state, adjoint, made = outputs(
        forward,
        backward,
        (seen, back, prefix_map, suffix_map, fresh, out, push, read, prefix, suffix),
        got,
    )
    z = gradients(ints, keys_got, others, gate, column, keys, y, state, adjoint, made)
    output, value_grad = unpack_outputs(to_heads(y))
    query_grad, key_grad, decay_grad, beta_grad = unpack_gradients(ints, to_heads(z))
    return (output, query_grad, key_grad, value_grad, decay_grad.T, beta_grad.T)


def solution(mesh):
    placed = (
        P(("ctx", "head"), None),
        P(("ctx", "head"), None),
        P(("ctx", "head"), None),
        P(("ctx", "head"), None),
        P(("ctx", "head"), None),
        P(),
        P(),
        P(),
        P(("ctx", "head"), None),
    )
    return jax.shard_map(
        local,
        mesh=mesh,
        in_specs=placed,
        out_specs=(P(("ctx", "head"), None),) * 6,
        check_vma=False,
    )
```

```python
import functools

import jax
import jax.numpy as jnp
from jax import lax
from jax.experimental import pallas as pl
from jax.experimental.pallas import tpu as pltpu
from jax.sharding import PartitionSpec as P

VALUE_HEAD_COUNT = 32
NK = 16
DK = 128
DV = 128
GROUP = 128
GATE_ROWS = 16
PACK_HEADS = 16
BLOCKS = 16
SHARDS = 8
GRADIENT_BLOCKS = 4
LATER_BLOCKS = 8
SMALL_VMEM = 24 * 1024 * 1024
LARGE_VMEM = 58 * 1024 * 1024

bf16 = jnp.bfloat16
f32 = jnp.float32


def contract(left, right, left_dim, right_dim):
    return lax.dot_general(
        left.astype(bf16),
        right.astype(bf16),
        (((left_dim,), (right_dim,)), ((), ())),
        preferred_element_type=f32,
    )


def mm(left, right):
    return contract(left, right, 1, 0)


def mm_nt(left, right):
    return contract(left, right, 1, 1)


def mm_tn(left, right):
    return contract(left, right, 0, 0)


def exact(left, right, left_dim, right_dim):
    return lax.dot_general(
        left,
        right,
        (((left_dim,), (right_dim,)), ((), ())),
        preferred_element_type=f32,
        precision=lax.Precision.HIGHEST,
    )


def iota(shape, dim):
    return lax.broadcasted_iota(jnp.int32, shape, dim)


def segment_of(positions, starts):
    count = jnp.zeros(positions.shape, jnp.int32)
    for start in starts:
        count = count + jnp.where(positions >= start, 1, 0)
    return count


def pick_column(table, block):
    lane = iota(table.shape, 1)
    return jnp.sum(jnp.where(lane == block, table, 0.0), axis=1, keepdims=True)


def block_gates(block, ints_ref, gate_ref, column_ref):
    starts = [ints_ref[1 + j] for j in range(4)]
    first = ints_ref[0] * 16 * GROUP + block * GROUP
    cum_row = gate_ref[0, pl.ds(block, 1), :]
    beta_row = gate_ref[1, pl.ds(block, 1), :]
    cum_col = pick_column(column_ref[0], block)
    beta_col = pick_column(column_ref[1], block)
    seg_row = segment_of(first + iota((1, GROUP), 1), starts)
    seg_col = segment_of(first + iota((GROUP, 1), 0), starts)
    before = segment_of(jnp.full((1, 1), first - 1, jnp.int32), starts)
    row, col = iota((GROUP, GROUP), 0), iota((GROUP, GROUP), 1)
    joined = (row >= col) & (seg_col == seg_row)
    spread = jnp.where(joined, cum_col - cum_row, 0.0)
    weighted = jnp.where(joined, jnp.exp(spread), 0.0) * beta_row
    entry = jnp.where(seg_col == before, jnp.exp(cum_col), 0.0)
    cum_last = cum_col[GROUP - 1 :, :]
    same_last = seg_col == seg_col[GROUP - 1 :, :]
    last = (
        jnp.where(same_last, jnp.exp(jnp.where(same_last, cum_last - cum_col, 0.0)), 0.0) * beta_col
    )
    return weighted, entry, last


def inverse_root(raw):
    return lax.rsqrt(jnp.sum(raw * raw, axis=1, keepdims=True) + 1e-06)


def block_rows(x_ref, local, part):
    return jnp.concatenate(
        [x_ref[2 * local + half, 64 * part : 64 * part + 64, :] for half in range(2)], axis=0
    )


def normed(x_ref, local):
    query_raw = block_rows(x_ref, local, 0).astype(f32)
    key_raw = block_rows(x_ref, local, 1).astype(f32)
    query_root, key_root = inverse_root(query_raw), inverse_root(key_raw)
    query = query_raw * query_root * DK ** (-0.5)
    keys = key_raw * key_root
    return query_raw, key_raw, query_root, key_root, query.astype(bf16), keys.astype(bf16)


def eye_of(size):
    return jnp.where(iota((size, size), 0) == iota((size, size), 1), 1.0, 0.0)


def cost(units):
    return pl.CostEstimate(
        flops=units * BLOCKS * 2 * 128**3 * 8, bytes_accessed=1 << 20, transcendentals=0
    )


def whole(*shape):
    return pl.BlockSpec(shape, lambda i: (0,) * len(shape))


def stepped(count, *shape):
    return pl.BlockSpec((count, *shape), lambda i: (i,) + (0,) * len(shape))


def triangular_inverses(stricts, row, col):
    differ = row ^ col
    eye = jnp.where(differ == 0, 1.0, 0.0)
    inverses = [eye - jnp.where(differ == 1, strict, 0.0) for strict in stricts]
    for level in range(1, 7):
        size = 1 << level
        band = (differ >= size) & (differ < 2 * size)
        held = [inverse.astype(bf16) for inverse in inverses]
        half = [
            mm(one, jnp.where(band, strict, 0.0)) for one, strict in zip(held, stricts)
        ]
        step = [mm(one, other) for one, other in zip(half, held)]
        inverses = [inverse - one for inverse, one in zip(inverses, step)]
    held = [inverse.astype(bf16) for inverse in inverses]
    upper = [strict.astype(bf16) for strict in stricts]
    lower = [(strict - one.astype(f32)).astype(bf16) for strict, one in zip(stricts, upper)]
    rest = [mm(one, other) for one, other in zip(upper, held)]
    fine = [mm(one, other) for one, other in zip(lower, held)]
    rest = [
        eye - one.astype(f32) - high - low for one, high, low in zip(held, rest, fine)
    ]
    return [one.astype(f32) + mm(one, other) for one, other in zip(held, rest)]


def tables_kernel(
    ints_ref,
    floats_ref,
    x_ref,
    send_ref,
    gate_ref,
    column_ref,
    inverse_ref,
    mixing_ref,
    keys_last_ref,
    fresh_ref,
    maps_ref,
    prefix_ref,
    prefix_free_ref,
    suffix_ref,
    suffix_free_ref,
):
    tail = x_ref[:, 256:, :].astype(f32)
    paired = tail.reshape(BLOCKS, 2, GATE_ROWS, 128)
    lane = iota((BLOCKS, GATE_ROWS, 128), 2)
    rows = iota((BLOCKS, GATE_ROWS, 128), 1)
    tail = jnp.where(lane < 64, paired[:, 0], paired[:, 1])
    decay_raw = jnp.sum(jnp.where(rows == 0, tail, 0.0), axis=1) + floats_ref[1]
    beta_raw = jnp.sum(jnp.where(rows == 1, tail, 0.0), axis=1)
    rate = -jnp.exp(jnp.full((BLOCKS, 128), floats_ref[0], f32))
    decay_log = rate * (jnp.maximum(decay_raw, 0.0) + jnp.log1p(jnp.exp(-jnp.abs(decay_raw))))
    row, col = iota((128, 128), 0), iota((128, 128), 1)
    eye = eye_of(128)
    cumulative = exact(decay_log, jnp.where(row <= col, 1.0, 0.0), 1, 0)
    beta = jax.nn.sigmoid(beta_raw)
    gate_ref[0] = cumulative
    gate_ref[1] = beta
    gate_ref[2] = rate * jax.nn.sigmoid(decay_raw)
    padding = jnp.zeros((128 - BLOCKS, 128), f32)
    column_ref[0] = exact(eye, jnp.concatenate([cumulative, padding], 0), 1, 1)
    column_ref[1] = exact(eye, jnp.concatenate([beta, padding], 0), 1, 1)

    each = range(BLOCKS)
    units = [normed(x_ref, i)[4:] for i in each]
    both = [mm_nt(jnp.concatenate([keys, query], 0), keys) for query, keys in units]
    gates = [block_gates(i, ints_ref, gate_ref, column_ref) for i in each]
    stricts = [jnp.where(row > col, gate[0] * one[:GROUP], 0.0) for gate, one in zip(gates, both)]
    mixing = [(gate[0] * one[GROUP:]).astype(bf16) for gate, one in zip(gates, both)]
    for i in each:
        mixing_ref[i] = mixing[i]
    inverses = [one.astype(bf16) for one in triangular_inverses(stricts, row, col)]
    keys_entry = [(units[i][1].astype(f32) * gates[i][1]).astype(bf16) for i in each]
    keys_last = [(units[i][1].astype(f32) * gates[i][2]).astype(bf16) for i in each]
    for i in each:
        inverse_ref[i] = inverses[i]
        keys_last_ref[i] = keys_last[i]
    pairs = [
        mm(inverses[i], jnp.concatenate([block_rows(x_ref, i, 2), keys_entry[i]], 1)).astype(bf16)
        for i in each
    ]
    seen = [pairs[i][:, DV:] for i in each]
    written = [mm_tn(keys_last[i], pairs[i]) for i in each]
    reads = [
        (gates[i][1] * units[i][0].astype(f32) - mm(mixing[i], seen[i])).astype(bf16) for i in each
    ]
    terms = [mm_tn(reads[i], block_rows(x_ref, i, 3)) for i in each]
    steps = [written[i][:, DV:].astype(bf16) for i in each]
    scales = [gates[i][1][GROUP - 1 :, :] for i in each]
    for i in each:
        fresh_ref[i] = pairs[i][:, :DV]
        maps_ref[i, 0] = seen[i]
        maps_ref[i, 1] = reads[i]
    nothing = jnp.zeros((DK, DK), f32)
    forward = jnp.concatenate([jnp.zeros((DK, DV), f32), eye], 1)
    backward = forward
    for i in each:
        other = BLOCKS - 1 - i
        forward_low, backward_low = forward.astype(bf16), backward.astype(bf16)
        prefix_free_ref[i] = forward_low[:, :DV]
        prefix_ref[i] = forward_low[:, DV:]
        suffix_free_ref[other] = backward_low[:, :DV]
        suffix_ref[other] = backward_low[:, DV:]
        forward = (
            scales[i] * forward
            - mm(steps[i], forward_low)
            + jnp.concatenate([written[i][:, :DV], nothing], 1)
        )
        backward = (
            scales[other] * backward
            - mm_tn(steps[other], backward_low)
            + jnp.concatenate([terms[other], nothing], 1)
        )
    total = forward[:, DV:].astype(bf16)
    for other in range(SHARDS):
        send_ref[other, :DK] = total
        send_ref[other, DK:] = jnp.where(
            ints_ref[0] < other, forward[:, :DV], backward[:, :DV]
        ).astype(bf16)


def tables(ints, floats, received):
    half = pltpu.HBM((BLOCKS, DK, DV), bf16)
    vmem = pl.BlockSpec(memory_space=pltpu.VMEM)
    smem = pl.BlockSpec(memory_space=pltpu.SMEM)
    return pl.pallas_call(
        tables_kernel,
        in_specs=[smem, smem, vmem],
        out_specs=[vmem] * 12,
        out_shape=[
            jax.ShapeDtypeStruct((SHARDS, 2 * DK, DV), bf16),
            pltpu.HBM((3, BLOCKS, 128), f32),
            pltpu.HBM((2, 128, 128), f32),
            *[half] * 4,
            pltpu.HBM((BLOCKS, 2, GROUP, DV), bf16),
            *[half] * 4,
        ],
        compiler_params=pltpu.CompilerParams(vmem_limit_bytes=SMALL_VMEM),
        cost_estimate=cost(30),
        name="tables",
    )(ints, floats, received)


def later_kernel(x_ref, inverse_ref, mixing_ref, keys_last_ref, fresh_ref, out_ref, push_ref, back_ref):
    each = range(LATER_BLOCKS)
    turned = [mm_tn(mixing_ref[i], block_rows(x_ref, i, 3)).astype(bf16) for i in each]
    outputs = [mm(mixing_ref[i], fresh_ref[i]) for i in each]
    pushed = [
        mm_tn(inverse_ref[i], jnp.concatenate([turned[i], keys_last_ref[i]], 1)).astype(bf16)
        for i in each
    ]
    for i in each:
        out_ref[i] = outputs[i].astype(bf16)
        push_ref[i] = pushed[i][:, :DV]
        back_ref[i] = pushed[i][:, DV:]


def later(received, inverse, mixing, keys_last, fresh):
    half = pltpu.HBM((BLOCKS, DK, DV), bf16)
    by_step = stepped(LATER_BLOCKS, GROUP, DV)
    return pl.pallas_call(
        later_kernel,
        grid=(BLOCKS // LATER_BLOCKS,),
        in_specs=[stepped(2 * LATER_BLOCKS, 256 + GATE_ROWS, 128)] + [by_step] * 4,
        out_specs=[by_step] * 3,
        out_shape=[half] * 3,
        compiler_params=pltpu.CompilerParams(vmem_limit_bytes=LARGE_VMEM),
        cost_estimate=cost(4),
        name="later",
    )(received, inverse, mixing, keys_last, fresh)


def split_two(state):
    high = state.astype(bf16)
    return jnp.concatenate([high, (state - high.astype(f32)).astype(bf16)], 1)


def gradients_kernel(
    ints_ref,
    x_ref,
    shards_ref,
    gate_ref,
    column_ref,
    out_ref,
    push_ref,
    back_ref,
    fresh_ref,
    maps_ref,
    prefix_ref,
    prefix_free_ref,
    suffix_ref,
    suffix_free_ref,
    y_ref,
    ends_ref,
):
    here = pl.program_id(0)

    @pl.when(here == 0)
    def prologue():
        me = ints_ref[0]
        state = jnp.zeros((DK, DV), f32)
        adjoint = jnp.zeros((DK, DV), f32)
        for k in range(7):
            moved = mm(shards_ref[k, :DK], split_two(state))
            new = moved[:, :DV] + moved[:, DV:] + shards_ref[k, DK:].astype(f32)
            state = jnp.where(k < me, new, state)
            at = 7 - k
            moved = mm_tn(shards_ref[at, :DK], split_two(adjoint))
            new = moved[:, :DV] + moved[:, DV:] + shards_ref[at, DK:].astype(f32)
            adjoint = jnp.where(at > me, new, adjoint)
        ends_ref[0] = state.astype(bf16)
        ends_ref[1] = adjoint.astype(bf16)

    lane = iota((GROUP, 8), 1)
    sublane = iota((8, GROUP), 0)
    change_cols = jnp.zeros((GROUP, 8), f32)
    beta_cols = jnp.zeros((GROUP, 8), f32)
    column_sums = jnp.zeros((8, GROUP), f32)
    each = range(GRADIENT_BLOCKS)
    row, col = iota((GROUP, GROUP), 0), iota((GROUP, GROUP), 1)
    states = [prefix_free_ref[i].astype(f32) + mm(prefix_ref[i], ends_ref[0]) for i in each]
    adjoints = [suffix_free_ref[i].astype(f32) + mm(suffix_ref[i], ends_ref[1]) for i in each]
    states_low = [one.astype(bf16) for one in states]
    adjoints_low = [one.astype(bf16) for one in adjoints]
    reads = [mm(maps_ref[i].reshape(2 * GROUP, DK), states_low[i]) for i in each]
    fresh = [(fresh_ref[i].astype(f32) - reads[i][:GROUP]).astype(bf16) for i in each]
    outputs = [out_ref[i].astype(f32) + reads[i][GROUP:] for i in each]
    pushed = [push_ref[i].astype(f32) + mm(back_ref[i], adjoints_low[i]) for i in each]
    norms = [normed(x_ref, i) for i in each]
    both = [mm_nt(jnp.concatenate([one[5], one[4]], 0), one[5]) for one in norms]
    sides = [
        jnp.concatenate([block_rows(x_ref, i, 3), pushed[i].astype(bf16)], 0) for i in each
    ]
    on_fresh = [mm_nt(sides[i], fresh[i]) for i in each]
    on_state = [mm_nt(sides[i], states_low[i]) for i in each]
    on_adjoint = [mm_nt(fresh[i], adjoints_low[i]) for i in each]
    gates = [
        block_gates(here * GRADIENT_BLOCKS + i, ints_ref, gate_ref, column_ref) for i in each
    ]
    mix_terms = [gates[i][0] * on_fresh[i][:GROUP] for i in each]
    key_terms = [jnp.where(row > col, -gates[i][0] * on_fresh[i][GROUP:], 0.0) for i in each]
    stacked = [
        jnp.concatenate([mix_terms[i].astype(bf16), key_terms[i].astype(bf16)], 0) for i in each
    ]
    direct = [mm(stacked[i], norms[i][5]) for i in each]
    turned = [
        mm_tn(stacked[i], jnp.concatenate([norms[i][4], norms[i][5]], 0)) for i in each
    ]
    for local in each:
        _, entry, last = gates[local]
        query_raw, key_raw, query_root, key_root, query, keys = norms[local]
        query_entry = entry * on_state[local][:GROUP]
        key_entry = -entry * on_state[local][GROUP:]
        key_last = last * on_adjoint[local]
        query_grad = query_entry + direct[local][:GROUP]
        key_grad = key_entry + key_last + direct[local][GROUP:] + turned[local]
        query_wide, key_wide = query.astype(f32), keys.astype(f32)
        table = mix_terms[local] * both[local][GROUP:] + key_terms[local] * both[local][:GROUP]
        last_sums = jnp.sum(key_wide * key_last, axis=1, keepdims=True)
        change = (
            jnp.sum(table + query_wide * query_entry + key_wide * key_entry, axis=1, keepdims=True)
            - last_sums
        )
        extra = jnp.sum(last_sums, axis=0, keepdims=True) + entry[GROUP - 1 :, :] * jnp.sum(
            jnp.sum(adjoints[local] * states[local], axis=0, keepdims=True), axis=1, keepdims=True
        )
        change = change + jnp.where(iota((GROUP, 1), 0) == GROUP - 1, extra, 0.0)
        change_cols = jnp.where(lane == local, change, change_cols)
        beta_cols = jnp.where(lane == local, last_sums, beta_cols)
        column_sums = jnp.where(
            sublane == local, jnp.sum(table, axis=0, keepdims=True), column_sums
        )
        query_grad = query_grad * DK ** (-0.5)
        query_dot = jnp.sum(query_grad * query_raw, axis=1, keepdims=True)
        key_dot = jnp.sum(key_grad * key_raw, axis=1, keepdims=True)
        query_back = query_root * query_grad - query_raw * (
            query_root * query_root * query_root * query_dot
        )
        key_back = key_root * key_grad - key_raw * (key_root * key_root * key_root * key_dot)
        for half in range(2):
            rows = slice(64 * half, 64 * half + 64)
            at = 2 * local + half
            y_ref[at, 0:64, :] = outputs[local][rows].astype(bf16)
            y_ref[at, 64:128, :] = query_back[rows].astype(bf16)
            y_ref[at, 128:192, :] = key_back[rows].astype(bf16)
            y_ref[at, 192:256, :] = pushed[local][rows].astype(bf16)

    after = jnp.where(row >= col, 1.0, 0.0)
    eye = jnp.where(row == col, 1.0, 0.0)
    decay_rows = exact(change_cols, after, 0, 0) - exact(column_sums, after, 1, 0)
    beta_rows = exact(beta_cols, eye, 0, 0) + column_sums
    for local in range(GRADIENT_BLOCKS):
        block = here * GRADIENT_BLOCKS + local
        decay_grad = decay_rows[local : local + 1] * gate_ref[2, pl.ds(block, 1), :]
        beta_grad = beta_rows[local : local + 1] * (1.0 - gate_ref[1, pl.ds(block, 1), :])
        rows = iota((GATE_ROWS, 128), 0)
        tail = jnp.where(rows == 0, decay_grad, jnp.where(rows == 1, beta_grad, 0.0)).astype(bf16)
        for half in range(2):
            y_ref[2 * local + half, 256:, :] = tail


def gradients(ints, received, shards, gate, column, *made):
    by_step = stepped(GRADIENT_BLOCKS, GROUP, DV)
    rows_spec = stepped(2 * GRADIENT_BLOCKS, 256 + GATE_ROWS, 128)
    return pl.pallas_call(
        gradients_kernel,
        grid=(BLOCKS // GRADIENT_BLOCKS,),
        in_specs=[
            pl.BlockSpec(memory_space=pltpu.SMEM),
            rows_spec,
            whole(SHARDS, 2 * DK, DV),
            whole(3, BLOCKS, 128),
            whole(2, 128, 128),
            *[by_step] * 4,
            stepped(GRADIENT_BLOCKS, 2, GROUP, DV),
            *[by_step] * 4,
        ],
        out_specs=rows_spec,
        out_shape=jax.ShapeDtypeStruct(received.shape, bf16),
        scratch_shapes=[pltpu.VMEM((2, DK, DV), bf16)],
        compiler_params=pltpu.CompilerParams(
            dimension_semantics=("arbitrary",), vmem_limit_bytes=LARGE_VMEM
        ),
        cost_estimate=cost(20),
        name="gradients",
    )(ints, received, shards, gate, column, *made)


def pack_kernel(query_ref, key_ref, value_ref, decay_ref, beta_ref, grad_ref, x_ref):
    decay = jnp.concatenate([decay_ref[...].astype(f32)] * 2, 1)
    beta = jnp.concatenate([beta_ref[...].astype(f32)] * 2, 1)
    rows = iota((GATE_ROWS, 128), 0)
    for head in range(PACK_HEADS):
        shared = slice(DK * (head // 2), DK * (head // 2) + DK)
        own = slice(DV * head, DV * head + DV)
        x_ref[head, 0:64, :] = query_ref[:, shared]
        x_ref[head, 64:128, :] = key_ref[:, shared]
        x_ref[head, 128:192, :] = value_ref[:, own]
        x_ref[head, 192:256, :] = grad_ref[:, own]
        x_ref[head, 256:, :] = jnp.where(
            rows == 0,
            decay[head : head + 1],
            jnp.where(rows == 1, beta[head : head + 1], 0.0),
        ).astype(bf16)


def pack(query, key, value, decay, beta, grad):
    wide = pl.BlockSpec((64, PACK_HEADS * DV), lambda i: (0, i))
    narrow = pl.BlockSpec((64, PACK_HEADS * DK // 2), lambda i: (0, i))
    gates = pl.BlockSpec((PACK_HEADS, 64), lambda i: (i, 0))
    return pl.pallas_call(
        pack_kernel,
        grid=(VALUE_HEAD_COUNT // PACK_HEADS,),
        in_specs=[narrow, narrow, wide, gates, gates, wide],
        out_specs=pl.BlockSpec((PACK_HEADS, 256 + GATE_ROWS, 128), lambda i: (i, 0, 0)),
        out_shape=jax.ShapeDtypeStruct((VALUE_HEAD_COUNT, 256 + GATE_ROWS, 128), bf16),
        compiler_params=pltpu.CompilerParams(vmem_limit_bytes=LARGE_VMEM),
        name="pack",
    )(query, key, value, decay, beta, grad)


def unpack_kernel(ints_ref, y_ref, out_ref, query_ref, key_ref, value_ref, decay_ref, beta_ref):
    for head in range(PACK_HEADS):
        own = slice(DV * head, DV * head + DV)
        out_ref[:, own] = y_ref[head, 0:64, :]
        value_ref[:, own] = y_ref[head, 192:256, :]
    for head in range(PACK_HEADS // 2):
        shared = slice(DK * head, DK * head + DK)
        for part, ref in ((1, query_ref), (2, key_ref)):
            rows = slice(64 * part, 64 * part + 64)
            summed = y_ref[2 * head, rows, :].astype(f32) + y_ref[2 * head + 1, rows, :].astype(f32)
            ref[:, shared] = summed.astype(bf16)
    tail = y_ref[:, 256:, :].astype(f32)
    rows = iota(tail.shape, 1)
    for index, ref in ((0, decay_ref), (1, beta_ref)):
        picked = jnp.sum(jnp.where(rows == index, tail, 0.0), axis=1)
        ref[...] = jnp.where(ints_ref[5] == 0, picked[:, :64], picked[:, 64:]).astype(bf16)


def unpack(ints, returned):
    wide = pl.BlockSpec((64, PACK_HEADS * DV), lambda i: (0, i))
    narrow = pl.BlockSpec((64, PACK_HEADS * DK // 2), lambda i: (0, i))
    gates = pl.BlockSpec((PACK_HEADS, 64), lambda i: (i, 0))
    wide_out = jax.ShapeDtypeStruct((64, VALUE_HEAD_COUNT * DV), bf16)
    narrow_out = jax.ShapeDtypeStruct((64, NK * DK), bf16)
    gates_out = jax.ShapeDtypeStruct((VALUE_HEAD_COUNT, 64), bf16)
    return pl.pallas_call(
        unpack_kernel,
        grid=(VALUE_HEAD_COUNT // PACK_HEADS,),
        in_specs=[
            pl.BlockSpec(memory_space=pltpu.SMEM),
            pl.BlockSpec((PACK_HEADS, 256 + GATE_ROWS, 128), lambda i: (i, 0, 0)),
        ],
        out_specs=[wide, narrow, narrow, wide, gates, gates],
        out_shape=[wide_out, narrow_out, narrow_out, wide_out, gates_out, gates_out],
        compiler_params=pltpu.CompilerParams(vmem_limit_bytes=SMALL_VMEM),
        name="unpack",
    )(ints, returned)


def local(
    query_raw,
    key_raw,
    value_raw,
    decay_raw,
    beta_raw,
    decay_base,
    decay_bias,
    doc_lengths,
    out_grad,
):
    head = lax.axis_index("head")
    shard = lax.axis_index("ctx")
    sent = pack(query_raw, key_raw, value_raw, decay_raw.T, beta_raw.T, out_grad)
    received = lax.all_to_all(sent, "head", split_axis=0, concat_axis=0, tiled=True)
    ends = [jnp.sum(doc_lengths[:j]) for j in range(4)]
    ints = jnp.stack([shard.astype(jnp.int32), *ends, (head % 2).astype(jnp.int32)])
    floats = jnp.stack(
        [
            lax.dynamic_index_in_dim(decay_base, head, keepdims=False),
            lax.dynamic_index_in_dim(decay_bias, head, keepdims=False),
        ]
    )
    send, gate, column, inverse, mixing, keys_last, fresh, *made = tables(ints, floats, received)
    shards = lax.all_to_all(send, "ctx", split_axis=0, concat_axis=0, tiled=True)
    out, push, turned = later(received, inverse, mixing, keys_last, fresh)
    back = gradients(ints, received, shards, gate, column, out, push, turned, fresh, *made)
    returned = lax.all_to_all(back, "head", split_axis=0, concat_axis=0, tiled=True)
    output, query_grad, key_grad, value_grad, decay_grad, beta_grad = unpack(ints, returned)
    return (output, query_grad, key_grad, value_grad, decay_grad.T, beta_grad.T)


def solution(mesh):
    placed = (
        P(("ctx", "head"), None),
        P(("ctx", "head"), None),
        P(("ctx", "head"), None),
        P(("ctx", "head"), None),
        P(("ctx", "head"), None),
        P(),
        P(),
        P(),
        P(("ctx", "head"), None),
    )
    return jax.shard_map(
        local,
        mesh=mesh,
        in_specs=placed,
        out_specs=(P(("ctx", "head"), None),) * 6,
        check_vma=False,
    )
```

```python
import functools

import jax
import jax.numpy as jnp
from jax import lax
from jax.experimental import pallas as pl
from jax.experimental.pallas import tpu as pltpu
from jax.sharding import PartitionSpec as P

VALUE_HEAD_COUNT = 32
NK = 16
DK = 128
DV = 128
GROUP = 128
GATE_ROWS = 8
PACK_HEADS = 16
BLOCKS = 16
SHARDS = 8
HELD = 12
GRADIENT_BLOCKS = 8
LATER_BLOCKS = 8
SMALL_VMEM = 24 * 1024 * 1024
LARGE_VMEM = 58 * 1024 * 1024

bf16 = jnp.bfloat16
f32 = jnp.float32


def contract(left, right, left_dim, right_dim):
    return lax.dot_general(
        left.astype(bf16),
        right.astype(bf16),
        (((left_dim,), (right_dim,)), ((), ())),
        preferred_element_type=f32,
    )


def mm(left, right):
    return contract(left, right, 1, 0)


def mm_nt(left, right):
    return contract(left, right, 1, 1)


def mm_tn(left, right):
    return contract(left, right, 0, 0)


def exact(left, right, left_dim, right_dim):
    return lax.dot_general(
        left,
        right,
        (((left_dim,), (right_dim,)), ((), ())),
        preferred_element_type=f32,
        precision=lax.Precision.HIGHEST,
    )


def iota(shape, dim):
    return lax.broadcasted_iota(jnp.int32, shape, dim)


def segment_of(positions, starts):
    count = jnp.zeros(positions.shape, jnp.int32)
    for start in starts:
        count = count + jnp.where(positions >= start, 1, 0)
    return count


def pick_column(table, block):
    lane = iota(table.shape, 1)
    return jnp.sum(jnp.where(lane == block, table, 0.0), axis=1, keepdims=True)


def token_tables(cumulative, beta, ints_ref):
    starts = [ints_ref[1 + j] for j in range(4)]
    row, block = iota((GROUP, 128), 0), iota((GROUP, 128), 1)
    first = ints_ref[0] * BLOCKS * GROUP + block * GROUP
    positions = first + row
    segment = segment_of(positions, starts)
    entry = jnp.where(segment == segment_of(first - 1, starts), jnp.exp(cumulative), 0.0)
    same = segment == segment_of(first + GROUP - 1, starts)
    spread = jnp.where(same, cumulative[GROUP - 1 :, :] - cumulative, 0.0)
    last = jnp.where(same, jnp.exp(spread), 0.0) * beta
    opened = jnp.zeros((GROUP, 128), jnp.int32)
    for start in starts:
        opened = jnp.where(positions >= start, start, opened)
    return entry, last, (opened - first).astype(f32)


def inverse_root(raw):
    return lax.rsqrt(jnp.sum(raw * raw, axis=1, keepdims=True) + 1e-06)


def block_rows(x_ref, local, part):
    return jnp.concatenate(
        [x_ref[2 * local + half, 64 * part : 64 * part + 64, :] for half in range(2)], axis=0
    )


def normed(x_ref, local):
    query_raw = block_rows(x_ref, local, 0).astype(f32)
    key_raw = block_rows(x_ref, local, 1).astype(f32)
    query_root, key_root = inverse_root(query_raw), inverse_root(key_raw)
    query = query_raw * query_root * DK ** (-0.5)
    keys = key_raw * key_root
    return query_raw, key_raw, query_root, key_root, query.astype(bf16), keys.astype(bf16)


def eye_of(size):
    return jnp.where(iota((size, size), 0) == iota((size, size), 1), 1.0, 0.0)


def cost(units):
    return pl.CostEstimate(
        flops=units * BLOCKS * 2 * 128**3 * 8, bytes_accessed=1 << 20, transcendentals=0
    )


def whole(*shape):
    return pl.BlockSpec(shape, lambda i: (0,) * len(shape))


def stepped(count, *shape):
    return pl.BlockSpec((count, *shape), lambda i: (i,) + (0,) * len(shape))


def triangular_inverses(stricts, row, col):
    differ = row ^ col
    eye = jnp.where(differ == 0, 1.0, 0.0)
    inverses = [eye - jnp.where(differ == 1, strict, 0.0) for strict in stricts]
    for level in range(1, 7):
        size = 1 << level
        band = (differ >= size) & (differ < 2 * size)
        held = [inverse.astype(bf16) for inverse in inverses]
        half = [
            mm(one, jnp.where(band, strict, 0.0)) for one, strict in zip(held, stricts)
        ]
        step = [mm(one, other) for one, other in zip(half, held)]
        inverses = [inverse - one for inverse, one in zip(inverses, step)]
    held = [inverse.astype(bf16) for inverse in inverses]
    upper = [strict.astype(bf16) for strict in stricts]
    lower = [(strict - one.astype(f32)).astype(bf16) for strict, one in zip(stricts, upper)]
    rest = [mm(one, other) for one, other in zip(upper, held)]
    fine = [mm(one, other) for one, other in zip(lower, held)]
    rest = [
        eye - one.astype(f32) - high - low for one, high, low in zip(held, rest, fine)
    ]
    return [one.astype(f32) + mm(one, other) for one, other in zip(held, rest)]


def tables_kernel(ints_ref, floats_ref, x_ref, send_ref, gate_ref, column_ref, *rest):
    outs, held, sems = rest[:HELD], rest[HELD : 2 * HELD], rest[2 * HELD]
    (
        weighted_ref,
        strict_ref,
        mixing_ref,
        inverse_ref,
        keys_last_ref,
        fresh_ref,
        seen_ref,
        read_ref,
        prefix_ref,
        prefix_free_ref,
        suffix_ref,
        suffix_free_ref,
    ) = held
    copies = [
        pltpu.make_async_copy(from_ref, to_ref, sems.at[k])
        for k, (from_ref, to_ref) in enumerate(zip(held, outs))
    ]
    tail = x_ref[:, 256:, :].astype(f32)
    paired = tail.reshape(BLOCKS, 2, GATE_ROWS, 128)
    lane = iota((BLOCKS, GATE_ROWS, 128), 2)
    rows = iota((BLOCKS, GATE_ROWS, 128), 1)
    tail = jnp.where(lane < 64, paired[:, 0], paired[:, 1])
    decay_raw = jnp.sum(jnp.where(rows == 0, tail, 0.0), axis=1) + floats_ref[1]
    beta_raw = jnp.sum(jnp.where(rows == 1, tail, 0.0), axis=1)
    rate = -jnp.exp(jnp.full((BLOCKS, 128), floats_ref[0], f32))
    decay_log = rate * (jnp.maximum(decay_raw, 0.0) + jnp.log1p(jnp.exp(-jnp.abs(decay_raw))))
    row, col = iota((128, 128), 0), iota((128, 128), 1)
    eye = eye_of(128)
    cumulative = exact(decay_log, jnp.where(row <= col, 1.0, 0.0), 1, 0)
    beta = jax.nn.sigmoid(beta_raw)
    gate_ref[0] = cumulative
    gate_ref[1] = beta
    gate_ref[2] = rate * jax.nn.sigmoid(decay_raw)
    padding = jnp.zeros((128 - BLOCKS, 128), f32)
    cum_cols = exact(eye, jnp.concatenate([cumulative, padding], 0), 1, 1)
    beta_cols = exact(eye, jnp.concatenate([beta, padding], 0), 1, 1)
    entry_cols, last_cols, opened_cols = token_tables(cum_cols, beta_cols, ints_ref)
    column_ref[0] = entry_cols
    column_ref[1] = last_cols

    each = range(BLOCKS)
    units = [normed(x_ref, i)[4:] for i in each]
    both = [mm_nt(jnp.concatenate([keys, query], 0), keys) for query, keys in units]
    wide_col = col.astype(f32)
    gates = []
    for i in each:
        joined = (row >= col) & (wide_col >= opened_cols[:, i : i + 1])
        spread = jnp.where(joined, cum_cols[:, i : i + 1] - cumulative[i : i + 1], 0.0)
        weighted = jnp.where(joined, jnp.exp(spread), 0.0) * beta[i : i + 1]
        gates.append((weighted, entry_cols[:, i : i + 1], last_cols[:, i : i + 1]))
        weighted_ref[i] = weighted.astype(bf16)
    stricts = [jnp.where(row > col, gate[0] * one[:GROUP], 0.0) for gate, one in zip(gates, both)]
    mixing = [(gate[0] * one[GROUP:]).astype(bf16) for gate, one in zip(gates, both)]
    for i in each:
        mixing_ref[i] = mixing[i]
        strict_ref[i] = stricts[i].astype(bf16)
    for k in range(0, 3):
        copies[k].start()
    inverses = [one.astype(bf16) for one in triangular_inverses(stricts, row, col)]
    keys_entry = [(units[i][1].astype(f32) * gates[i][1]).astype(bf16) for i in each]
    keys_last = [(units[i][1].astype(f32) * gates[i][2]).astype(bf16) for i in each]
    for i in each:
        inverse_ref[i] = inverses[i]
        keys_last_ref[i] = keys_last[i]
    for k in range(3, 5):
        copies[k].start()
    pairs = [
        mm(inverses[i], jnp.concatenate([block_rows(x_ref, i, 2), keys_entry[i]], 1)).astype(bf16)
        for i in each
    ]
    seen = [pairs[i][:, DV:] for i in each]
    written = [mm_tn(keys_last[i], pairs[i]) for i in each]
    reads = [
        (gates[i][1] * units[i][0].astype(f32) - mm(mixing[i], seen[i])).astype(bf16) for i in each
    ]
    terms = [mm_tn(reads[i], block_rows(x_ref, i, 3)) for i in each]
    steps = [written[i][:, DV:].astype(bf16) for i in each]
    scales = [gates[i][1][GROUP - 1 :, :] for i in each]
    for i in each:
        fresh_ref[i] = pairs[i][:, :DV]
        seen_ref[i] = seen[i]
        read_ref[i] = reads[i]
    for k in range(5, 8):
        copies[k].start()
    nothing = jnp.zeros((DK, DK), f32)
    initial = jnp.concatenate([jnp.zeros((DK, DV), f32), eye], 1)

    def advance(i, state):
        return (
            scales[i] * state
            - mm(steps[i], state)
            + jnp.concatenate([written[i][:, :DV], nothing], 1)
        )

    def retreat(i, state):
        return (
            scales[i] * state
            - mm_tn(steps[i], state)
            + jnp.concatenate([terms[i], nothing], 1)
        )

    middle = BLOCKS // 2
    lows, highs = [initial], [initial]
    low_ends, high_ends = [initial], [initial]
    for i in range(middle):
        lows.append(advance(i, lows[-1]))
        highs.append(advance(middle + i, highs[-1]))
        high_ends.append(retreat(BLOCKS - 1 - i, high_ends[-1]))
        low_ends.append(retreat(middle - 1 - i, low_ends[-1]))

    def joined_states(later_states, entry_state):
        moved = [mm(one[:, DV:], entry_state) for one in later_states]
        return [
            one + jnp.concatenate([later_one[:, :DV], nothing], 1)
            for one, later_one in zip(moved, later_states)
        ]

    forwards = lows[:middle] + joined_states(highs, lows[middle])
    backwards = high_ends[:middle] + joined_states(low_ends, high_ends[middle])
    for i in each:
        other = BLOCKS - 1 - i
        prefix_free_ref[i] = forwards[i][:, :DV].astype(bf16)
        prefix_ref[i] = forwards[i][:, DV:].astype(bf16)
        suffix_free_ref[other] = backwards[i][:, :DV].astype(bf16)
        suffix_ref[other] = backwards[i][:, DV:].astype(bf16)
    forward, backward = forwards[BLOCKS], backwards[BLOCKS]
    for k in range(8, HELD):
        copies[k].start()
    total = forward[:, DV:].astype(bf16)
    for other in range(SHARDS):
        send_ref[other, :DK] = total
        send_ref[other, DK:] = jnp.where(
            ints_ref[0] < other, forward[:, :DV], backward[:, :DV]
        ).astype(bf16)
    for copy in copies:
        copy.wait()


def tables(ints, floats, received):
    half = pltpu.HBM((BLOCKS, DK, DV), bf16)
    vmem = pl.BlockSpec(memory_space=pltpu.VMEM)
    smem = pl.BlockSpec(memory_space=pltpu.SMEM)
    return pl.pallas_call(
        tables_kernel,
        in_specs=[smem, smem, vmem],
        out_specs=[vmem] * 3 + [pl.BlockSpec(memory_space=pl.ANY)] * HELD,
        out_shape=[
            jax.ShapeDtypeStruct((SHARDS, 2 * DK, DV), bf16),
            pltpu.HBM((3, BLOCKS, 128), f32),
            pltpu.HBM((2, 128, 128), f32),
            *[half] * HELD,
        ],
        scratch_shapes=[pltpu.VMEM((BLOCKS, DK, DV), bf16)] * HELD
        + [pltpu.SemaphoreType.DMA((HELD,))],
        compiler_params=pltpu.CompilerParams(vmem_limit_bytes=SMALL_VMEM),
        cost_estimate=cost(30),
        name="tables",
    )(ints, floats, received)


def later_kernel(x_ref, inverse_ref, mixing_ref, keys_last_ref, fresh_ref, out_ref, push_ref, back_ref):
    each = range(LATER_BLOCKS)
    turned = [mm_tn(mixing_ref[i], block_rows(x_ref, i, 3)).astype(bf16) for i in each]
    outputs = [mm(mixing_ref[i], fresh_ref[i]) for i in each]
    pushed = [
        mm_tn(inverse_ref[i], jnp.concatenate([turned[i], keys_last_ref[i]], 1)).astype(bf16)
        for i in each
    ]
    for i in each:
        out_ref[i] = outputs[i].astype(bf16)
        push_ref[i] = pushed[i][:, :DV]
        back_ref[i] = pushed[i][:, DV:]


def later(received, inverse, mixing, keys_last, fresh):
    half = pltpu.HBM((BLOCKS, DK, DV), bf16)
    by_step = stepped(LATER_BLOCKS, GROUP, DV)
    return pl.pallas_call(
        later_kernel,
        grid=(BLOCKS // LATER_BLOCKS,),
        in_specs=[stepped(2 * LATER_BLOCKS, 256 + GATE_ROWS, 128)] + [by_step] * 4,
        out_specs=[by_step] * 3,
        out_shape=[half] * 3,
        compiler_params=pltpu.CompilerParams(vmem_limit_bytes=LARGE_VMEM),
        cost_estimate=cost(4),
        name="later",
    )(received, inverse, mixing, keys_last, fresh)


def split_two(state):
    high = state.astype(bf16)
    return jnp.concatenate([high, (state - high.astype(f32)).astype(bf16)], 1)


def gradients_kernel(
    ints_ref,
    x_ref,
    shards_ref,
    gate_ref,
    column_ref,
    out_ref,
    push_ref,
    back_ref,
    weighted_ref,
    strict_ref,
    mixing_ref,
    fresh_ref,
    seen_ref,
    read_ref,
    prefix_ref,
    prefix_free_ref,
    suffix_ref,
    suffix_free_ref,
    y_ref,
    ends_ref,
):
    here = pl.program_id(0)

    @pl.when(here == 0)
    def prologue():
        me = ints_ref[0]
        state = jnp.zeros((DK, DV), f32)
        adjoint = jnp.zeros((DK, DV), f32)
        for k in range(7):
            moved = mm(shards_ref[k, :DK], split_two(state))
            new = moved[:, :DV] + moved[:, DV:] + shards_ref[k, DK:].astype(f32)
            state = jnp.where(k < me, new, state)
            at = 7 - k
            moved = mm_tn(shards_ref[at, :DK], split_two(adjoint))
            new = moved[:, :DV] + moved[:, DV:] + shards_ref[at, DK:].astype(f32)
            adjoint = jnp.where(at > me, new, adjoint)
        ends_ref[0] = state.astype(bf16)
        ends_ref[1] = adjoint.astype(bf16)

    lane = iota((GROUP, 8), 1)
    sublane = iota((8, GROUP), 0)
    change_cols = jnp.zeros((GROUP, 8), f32)
    beta_cols = jnp.zeros((GROUP, 8), f32)
    column_sums = jnp.zeros((8, GROUP), f32)
    each = range(GRADIENT_BLOCKS)
    row, col = iota((GROUP, GROUP), 0), iota((GROUP, GROUP), 1)
    states = [prefix_free_ref[i].astype(f32) + mm(prefix_ref[i], ends_ref[0]) for i in each]
    adjoints = [suffix_free_ref[i].astype(f32) + mm(suffix_ref[i], ends_ref[1]) for i in each]
    states_low = [one.astype(bf16) for one in states]
    adjoints_low = [one.astype(bf16) for one in adjoints]
    fresh = [
        (fresh_ref[i].astype(f32) - mm(seen_ref[i], states_low[i])).astype(bf16) for i in each
    ]
    outputs = [out_ref[i].astype(f32) + mm(read_ref[i], states_low[i]) for i in each]
    pushed = [push_ref[i].astype(f32) + mm(back_ref[i], adjoints_low[i]) for i in each]
    norms = [normed(x_ref, i) for i in each]
    sides = [
        jnp.concatenate([block_rows(x_ref, i, 3), pushed[i].astype(bf16)], 0) for i in each
    ]
    on_fresh = [mm_nt(sides[i], fresh[i]) for i in each]
    on_state = [mm_nt(sides[i], states_low[i]) for i in each]
    on_adjoint = [mm_nt(fresh[i], adjoints_low[i]) for i in each]
    mix_terms = [weighted_ref[i].astype(f32) * on_fresh[i][:GROUP] for i in each]
    key_terms = [
        jnp.where(row > col, -weighted_ref[i].astype(f32) * on_fresh[i][GROUP:], 0.0) for i in each
    ]
    stacked = [
        jnp.concatenate([mix_terms[i].astype(bf16), key_terms[i].astype(bf16)], 0) for i in each
    ]
    direct = [mm(stacked[i], norms[i][5]) for i in each]
    turned = [
        mm_tn(stacked[i], jnp.concatenate([norms[i][4], norms[i][5]], 0)) for i in each
    ]
    for local in each:
        block = here * GRADIENT_BLOCKS + local
        entry, last = pick_column(column_ref[0], block), pick_column(column_ref[1], block)
        query_raw, key_raw, query_root, key_root, query, keys = norms[local]
        query_entry = entry * on_state[local][:GROUP]
        key_entry = -entry * on_state[local][GROUP:]
        key_last = last * on_adjoint[local]
        query_grad = query_entry + direct[local][:GROUP]
        key_grad = key_entry + key_last + direct[local][GROUP:] + turned[local]
        query_wide, key_wide = query.astype(f32), keys.astype(f32)
        table = (
            on_fresh[local][:GROUP] * mixing_ref[local].astype(f32)
            - on_fresh[local][GROUP:] * strict_ref[local].astype(f32)
        )
        last_sums = jnp.sum(key_wide * key_last, axis=1, keepdims=True)
        change = (
            jnp.sum(table + query_wide * query_entry + key_wide * key_entry, axis=1, keepdims=True)
            - last_sums
        )
        extra = jnp.sum(last_sums, axis=0, keepdims=True) + entry[GROUP - 1 :, :] * jnp.sum(
            jnp.sum(adjoints[local] * states[local], axis=0, keepdims=True), axis=1, keepdims=True
        )
        change = change + jnp.where(iota((GROUP, 1), 0) == GROUP - 1, extra, 0.0)
        change_cols = jnp.where(lane == local, change, change_cols)
        beta_cols = jnp.where(lane == local, last_sums, beta_cols)
        column_sums = jnp.where(
            sublane == local, jnp.sum(table, axis=0, keepdims=True), column_sums
        )
        query_grad = query_grad * DK ** (-0.5)
        query_dot = jnp.sum(query_grad * query_raw, axis=1, keepdims=True)
        key_dot = jnp.sum(key_grad * key_raw, axis=1, keepdims=True)
        query_back = query_root * query_grad - query_raw * (
            query_root * query_root * query_root * query_dot
        )
        key_back = key_root * key_grad - key_raw * (key_root * key_root * key_root * key_dot)
        for half in range(2):
            rows = slice(64 * half, 64 * half + 64)
            at = 2 * local + half
            y_ref[at, 0:64, :] = outputs[local][rows].astype(bf16)
            y_ref[at, 64:128, :] = query_back[rows].astype(bf16)
            y_ref[at, 128:192, :] = key_back[rows].astype(bf16)
            y_ref[at, 192:256, :] = pushed[local][rows].astype(bf16)

    after = jnp.where(row >= col, 1.0, 0.0)
    eye = jnp.where(row == col, 1.0, 0.0)
    decay_rows = exact(change_cols, after, 0, 0) - exact(column_sums, after, 1, 0)
    beta_rows = exact(beta_cols, eye, 0, 0) + column_sums
    for local in range(GRADIENT_BLOCKS):
        block = here * GRADIENT_BLOCKS + local
        decay_grad = decay_rows[local : local + 1] * gate_ref[2, pl.ds(block, 1), :]
        beta_grad = beta_rows[local : local + 1] * (1.0 - gate_ref[1, pl.ds(block, 1), :])
        rows = iota((GATE_ROWS, 128), 0)
        tail = jnp.where(rows == 0, decay_grad, jnp.where(rows == 1, beta_grad, 0.0)).astype(bf16)
        for half in range(2):
            y_ref[2 * local + half, 256:, :] = tail


def gradients(ints, received, shards, gate, column, *made):
    by_step = stepped(GRADIENT_BLOCKS, GROUP, DV)
    rows_spec = stepped(2 * GRADIENT_BLOCKS, 256 + GATE_ROWS, 128)
    return pl.pallas_call(
        gradients_kernel,
        grid=(BLOCKS // GRADIENT_BLOCKS,),
        in_specs=[
            pl.BlockSpec(memory_space=pltpu.SMEM),
            rows_spec,
            whole(SHARDS, 2 * DK, DV),
            whole(3, BLOCKS, 128),
            whole(2, 128, 128),
            *[by_step] * 13,
        ],
        out_specs=rows_spec,
        out_shape=jax.ShapeDtypeStruct(received.shape, bf16),
        scratch_shapes=[pltpu.VMEM((2, DK, DV), bf16)],
        compiler_params=pltpu.CompilerParams(
            dimension_semantics=("arbitrary",), vmem_limit_bytes=LARGE_VMEM
        ),
        cost_estimate=cost(20),
        name="gradients",
    )(ints, received, shards, gate, column, *made)


def pack_kernel(query_ref, key_ref, value_ref, decay_ref, beta_ref, grad_ref, x_ref):
    decay = jnp.concatenate([decay_ref[...].astype(f32)] * 2, 1)
    beta = jnp.concatenate([beta_ref[...].astype(f32)] * 2, 1)
    rows = iota((GATE_ROWS, 128), 0)
    for head in range(PACK_HEADS):
        shared = slice(DK * (head // 2), DK * (head // 2) + DK)
        own = slice(DV * head, DV * head + DV)
        x_ref[head, 0:64, :] = query_ref[:, shared]
        x_ref[head, 64:128, :] = key_ref[:, shared]
        x_ref[head, 128:192, :] = value_ref[:, own]
        x_ref[head, 192:256, :] = grad_ref[:, own]
        x_ref[head, 256:, :] = jnp.where(
            rows == 0,
            decay[head : head + 1],
            jnp.where(rows == 1, beta[head : head + 1], 0.0),
        ).astype(bf16)


def pack(query, key, value, decay, beta, grad):
    wide = pl.BlockSpec((64, PACK_HEADS * DV), lambda i: (0, i))
    narrow = pl.BlockSpec((64, PACK_HEADS * DK // 2), lambda i: (0, i))
    gates = pl.BlockSpec((PACK_HEADS, 64), lambda i: (i, 0))
    return pl.pallas_call(
        pack_kernel,
        grid=(VALUE_HEAD_COUNT // PACK_HEADS,),
        in_specs=[narrow, narrow, wide, gates, gates, wide],
        out_specs=pl.BlockSpec((PACK_HEADS, 256 + GATE_ROWS, 128), lambda i: (i, 0, 0)),
        out_shape=jax.ShapeDtypeStruct((VALUE_HEAD_COUNT, 256 + GATE_ROWS, 128), bf16),
        compiler_params=pltpu.CompilerParams(vmem_limit_bytes=LARGE_VMEM),
        name="pack",
    )(query, key, value, decay, beta, grad)


def unpack_kernel(ints_ref, y_ref, out_ref, query_ref, key_ref, value_ref, decay_ref, beta_ref):
    for head in range(PACK_HEADS):
        own = slice(DV * head, DV * head + DV)
        out_ref[:, own] = y_ref[head, 0:64, :]
        value_ref[:, own] = y_ref[head, 192:256, :]
    for head in range(PACK_HEADS // 2):
        shared = slice(DK * head, DK * head + DK)
        for part, ref in ((1, query_ref), (2, key_ref)):
            rows = slice(64 * part, 64 * part + 64)
            summed = y_ref[2 * head, rows, :].astype(f32) + y_ref[2 * head + 1, rows, :].astype(f32)
            ref[:, shared] = summed.astype(bf16)
    tail = y_ref[:, 256:, :].astype(f32)
    rows = iota(tail.shape, 1)
    for index, ref in ((0, decay_ref), (1, beta_ref)):
        picked = jnp.sum(jnp.where(rows == index, tail, 0.0), axis=1)
        ref[...] = jnp.where(ints_ref[5] == 0, picked[:, :64], picked[:, 64:]).astype(bf16)


def unpack(ints, returned):
    wide = pl.BlockSpec((64, PACK_HEADS * DV), lambda i: (0, i))
    narrow = pl.BlockSpec((64, PACK_HEADS * DK // 2), lambda i: (0, i))
    gates = pl.BlockSpec((PACK_HEADS, 64), lambda i: (i, 0))
    wide_out = jax.ShapeDtypeStruct((64, VALUE_HEAD_COUNT * DV), bf16)
    narrow_out = jax.ShapeDtypeStruct((64, NK * DK), bf16)
    gates_out = jax.ShapeDtypeStruct((VALUE_HEAD_COUNT, 64), bf16)
    return pl.pallas_call(
        unpack_kernel,
        grid=(VALUE_HEAD_COUNT // PACK_HEADS,),
        in_specs=[
            pl.BlockSpec(memory_space=pltpu.SMEM),
            pl.BlockSpec((PACK_HEADS, 256 + GATE_ROWS, 128), lambda i: (i, 0, 0)),
        ],
        out_specs=[wide, narrow, narrow, wide, gates, gates],
        out_shape=[wide_out, narrow_out, narrow_out, wide_out, gates_out, gates_out],
        compiler_params=pltpu.CompilerParams(vmem_limit_bytes=SMALL_VMEM),
        name="unpack",
    )(ints, returned)


def local(
    query_raw,
    key_raw,
    value_raw,
    decay_raw,
    beta_raw,
    decay_base,
    decay_bias,
    doc_lengths,
    out_grad,
):
    head = lax.axis_index("head")
    shard = lax.axis_index("ctx")
    sent = pack(query_raw, key_raw, value_raw, decay_raw.T, beta_raw.T, out_grad)
    received = lax.all_to_all(sent, "head", split_axis=0, concat_axis=0, tiled=True)
    ends = [jnp.sum(doc_lengths[:j]) for j in range(4)]
    ints = jnp.stack([shard.astype(jnp.int32), *ends, (head % 2).astype(jnp.int32)])
    floats = jnp.stack(
        [
            lax.dynamic_index_in_dim(decay_base, head, keepdims=False),
            lax.dynamic_index_in_dim(decay_bias, head, keepdims=False),
        ]
    )
    send, gate, column, weighted, strict, mixing, inverse, keys_last, fresh, *made = tables(
        ints, floats, received
    )
    shards = lax.all_to_all(send, "ctx", split_axis=0, concat_axis=0, tiled=True)
    out, push, turned = later(received, inverse, mixing, keys_last, fresh)
    back = gradients(
        ints, received, shards, gate, column, out, push, turned, weighted, strict, mixing, fresh, *made
    )
    returned = lax.all_to_all(back, "head", split_axis=0, concat_axis=0, tiled=True)
    output, query_grad, key_grad, value_grad, decay_grad, beta_grad = unpack(ints, returned)
    return (output, query_grad, key_grad, value_grad, decay_grad.T, beta_grad.T)


def solution(mesh):
    placed = (
        P(("ctx", "head"), None),
        P(("ctx", "head"), None),
        P(("ctx", "head"), None),
        P(("ctx", "head"), None),
        P(("ctx", "head"), None),
        P(),
        P(),
        P(),
        P(("ctx", "head"), None),
    )
    return jax.shard_map(
        local,
        mesh=mesh,
        in_specs=placed,
        out_specs=(P(("ctx", "head"), None),) * 6,
        check_vma=False,
    )
```

```python
import functools

import jax
import jax.numpy as jnp
from jax import lax
from jax.experimental import pallas as pl
from jax.experimental.pallas import tpu as pltpu
from jax.sharding import PartitionSpec as P

VALUE_HEAD_COUNT = 32
NK = 16
DK = 128
DV = 128
GROUP = 128
GATE_ROWS = 16
PACK_HEADS = 16
BLOCKS = 16
SHARDS = 8
HELD = 12
GRADIENT_BLOCKS = 8
LATER_BLOCKS = 8
SMALL_VMEM = 24 * 1024 * 1024
LARGE_VMEM = 58 * 1024 * 1024
GRADIENT_VMEM = 53 * 1024 * 1024

bf16 = jnp.bfloat16
f32 = jnp.float32


def contract(left, right, left_dim, right_dim):
    return lax.dot_general(
        left.astype(bf16),
        right.astype(bf16),
        (((left_dim,), (right_dim,)), ((), ())),
        preferred_element_type=f32,
    )


def mm(left, right):
    return contract(left, right, 1, 0)


def mm_nt(left, right):
    return contract(left, right, 1, 1)


def mm_tn(left, right):
    return contract(left, right, 0, 0)


def exact(left, right, left_dim, right_dim):
    return lax.dot_general(
        left,
        right,
        (((left_dim,), (right_dim,)), ((), ())),
        preferred_element_type=f32,
        precision=lax.Precision.HIGHEST,
    )


def iota(shape, dim):
    return lax.broadcasted_iota(jnp.int32, shape, dim)


def segment_of(positions, starts):
    count = jnp.zeros(positions.shape, jnp.int32)
    for start in starts:
        count = count + jnp.where(positions >= start, 1, 0)
    return count


def pick_column(table, block):
    lane = iota(table.shape, 1)
    return jnp.sum(jnp.where(lane == block, table, 0.0), axis=1, keepdims=True)


def token_tables(cumulative, beta, ints_ref):
    starts = [ints_ref[1 + j] for j in range(4)]
    row, block = iota((GROUP, 128), 0), iota((GROUP, 128), 1)
    first = ints_ref[0] * BLOCKS * GROUP + block * GROUP
    positions = first + row
    segment = segment_of(positions, starts)
    entry = jnp.where(segment == segment_of(first - 1, starts), jnp.exp(cumulative), 0.0)
    same = segment == segment_of(first + GROUP - 1, starts)
    spread = jnp.where(same, cumulative[GROUP - 1 :, :] - cumulative, 0.0)
    last = jnp.where(same, jnp.exp(spread), 0.0) * beta
    opened = jnp.zeros((GROUP, 128), jnp.int32)
    for start in starts:
        opened = jnp.where(positions >= start, start, opened)
    return entry, last, (opened - first).astype(f32)


def inverse_root(raw):
    return lax.rsqrt(jnp.sum(raw * raw, axis=1, keepdims=True) + 1e-06)


def block_rows(x_ref, local, part):
    return jnp.concatenate(
        [x_ref[2 * local + half, 64 * part : 64 * part + 64, :] for half in range(2)], axis=0
    )


def normed(x_ref, local):
    query_raw = block_rows(x_ref, local, 0).astype(f32)
    key_raw = block_rows(x_ref, local, 1).astype(f32)
    query_root, key_root = inverse_root(query_raw), inverse_root(key_raw)
    query = query_raw * query_root * DK ** (-0.5)
    keys = key_raw * key_root
    return query_raw, key_raw, query_root, key_root, query.astype(bf16), keys.astype(bf16)


def eye_of(size):
    return jnp.where(iota((size, size), 0) == iota((size, size), 1), 1.0, 0.0)


def cost(units):
    return pl.CostEstimate(
        flops=units * BLOCKS * 2 * 128**3 * 8, bytes_accessed=1 << 20, transcendentals=0
    )


def whole(*shape):
    return pl.BlockSpec(shape, lambda i: (0,) * len(shape))


def stepped(count, *shape):
    return pl.BlockSpec((count, *shape), lambda i: (i,) + (0,) * len(shape))


def triangular_inverses(stricts, row, col):
    differ = row ^ col
    eye = jnp.where(differ == 0, 1.0, 0.0)
    inverses = [eye - jnp.where(differ == 1, strict, 0.0) for strict in stricts]
    for level in range(1, 7):
        size = 1 << level
        band = (differ >= size) & (differ < 2 * size)
        held = [inverse.astype(bf16) for inverse in inverses]
        half = [
            mm(one, jnp.where(band, strict, 0.0)) for one, strict in zip(held, stricts)
        ]
        step = [mm(one, other) for one, other in zip(half, held)]
        inverses = [inverse - one for inverse, one in zip(inverses, step)]
    held = [inverse.astype(bf16) for inverse in inverses]
    upper = [strict.astype(bf16) for strict in stricts]
    lower = [(strict - one.astype(f32)).astype(bf16) for strict, one in zip(stricts, upper)]
    rest = [mm(one, other) for one, other in zip(upper, held)]
    fine = [mm(one, other) for one, other in zip(lower, held)]
    rest = [
        eye - one.astype(f32) - high - low for one, high, low in zip(held, rest, fine)
    ]
    return [one.astype(f32) + mm(one, other) for one, other in zip(held, rest)]


def tables_kernel(ints_ref, floats_ref, x_ref, send_ref, gate_ref, column_ref, *rest):
    outs, held, sems = rest[:HELD], rest[HELD : 2 * HELD], rest[2 * HELD]
    (
        weighted_ref,
        strict_ref,
        mixing_ref,
        inverse_ref,
        keys_last_ref,
        fresh_ref,
        seen_ref,
        read_ref,
        prefix_ref,
        prefix_free_ref,
        suffix_ref,
        suffix_free_ref,
    ) = held
    copies = [
        pltpu.make_async_copy(from_ref, to_ref, sems.at[k])
        for k, (from_ref, to_ref) in enumerate(zip(held, outs))
    ]
    tail = x_ref[:, 256:, :].astype(f32)
    paired = tail.reshape(BLOCKS, 2, GATE_ROWS, 128)
    lane = iota((BLOCKS, GATE_ROWS, 128), 2)
    rows = iota((BLOCKS, GATE_ROWS, 128), 1)
    tail = jnp.where(lane < 64, paired[:, 0], paired[:, 1])
    decay_raw = jnp.sum(jnp.where(rows == 0, tail, 0.0), axis=1) + floats_ref[1]
    beta_raw = jnp.sum(jnp.where(rows == 1, tail, 0.0), axis=1)
    rate = -jnp.exp(jnp.full((BLOCKS, 128), floats_ref[0], f32))
    decay_log = rate * (jnp.maximum(decay_raw, 0.0) + jnp.log1p(jnp.exp(-jnp.abs(decay_raw))))
    row, col = iota((128, 128), 0), iota((128, 128), 1)
    eye = eye_of(128)
    cumulative = exact(decay_log, jnp.where(row <= col, 1.0, 0.0), 1, 0)
    beta = jax.nn.sigmoid(beta_raw)
    gate_ref[0] = cumulative
    gate_ref[1] = beta
    gate_ref[2] = rate * jax.nn.sigmoid(decay_raw)
    padding = jnp.zeros((128 - BLOCKS, 128), f32)
    cum_cols = exact(eye, jnp.concatenate([cumulative, padding], 0), 1, 1)
    beta_cols = exact(eye, jnp.concatenate([beta, padding], 0), 1, 1)
    entry_cols, last_cols, opened_cols = token_tables(cum_cols, beta_cols, ints_ref)
    column_ref[0] = entry_cols
    column_ref[1] = last_cols

    each = range(BLOCKS)
    units = [normed(x_ref, i)[4:] for i in each]
    both = [mm_nt(jnp.concatenate([keys, query], 0), keys) for query, keys in units]
    wide_col = col.astype(f32)
    gates = []
    for i in each:
        joined = (row >= col) & (wide_col >= opened_cols[:, i : i + 1])
        spread = jnp.where(joined, cum_cols[:, i : i + 1] - cumulative[i : i + 1], 0.0)
        weighted = jnp.where(joined, jnp.exp(spread), 0.0) * beta[i : i + 1]
        gates.append((weighted, entry_cols[:, i : i + 1], last_cols[:, i : i + 1]))
        weighted_ref[i] = weighted.astype(bf16)
    stricts = [jnp.where(row > col, gate[0] * one[:GROUP], 0.0) for gate, one in zip(gates, both)]
    mixing = [(gate[0] * one[GROUP:]).astype(bf16) for gate, one in zip(gates, both)]
    for i in each:
        mixing_ref[i] = mixing[i]
        strict_ref[i] = stricts[i].astype(bf16)
    for k in range(0, 3):
        copies[k].start()
    inverses = [one.astype(bf16) for one in triangular_inverses(stricts, row, col)]
    keys_entry = [(units[i][1].astype(f32) * gates[i][1]).astype(bf16) for i in each]
    keys_last = [(units[i][1].astype(f32) * gates[i][2]).astype(bf16) for i in each]
    for i in each:
        inverse_ref[i] = inverses[i]
        keys_last_ref[i] = keys_last[i]
    for k in range(3, 5):
        copies[k].start()
    pairs = [
        mm(inverses[i], jnp.concatenate([block_rows(x_ref, i, 2), keys_entry[i]], 1)).astype(bf16)
        for i in each
    ]
    seen = [pairs[i][:, DV:] for i in each]
    written = [mm_tn(keys_last[i], pairs[i]) for i in each]
    reads = [
        (gates[i][1] * units[i][0].astype(f32) - mm(mixing[i], seen[i])).astype(bf16) for i in each
    ]
    terms = [mm_tn(reads[i], block_rows(x_ref, i, 3)) for i in each]
    steps = [written[i][:, DV:].astype(bf16) for i in each]
    scales = [gates[i][1][GROUP - 1 :, :] for i in each]
    for i in each:
        fresh_ref[i] = pairs[i][:, :DV]
        seen_ref[i] = seen[i]
        read_ref[i] = reads[i]
    for k in range(5, 8):
        copies[k].start()
    nothing = jnp.zeros((DK, DK), f32)
    initial = jnp.concatenate([jnp.zeros((DK, DV), f32), eye], 1)

    def advance(i, state):
        return (
            scales[i] * state
            - mm(steps[i], state)
            + jnp.concatenate([written[i][:, :DV], nothing], 1)
        )

    def retreat(i, state):
        return (
            scales[i] * state
            - mm_tn(steps[i], state)
            + jnp.concatenate([terms[i], nothing], 1)
        )

    middle = BLOCKS // 2
    lows, highs = [initial], [initial]
    low_ends, high_ends = [initial], [initial]
    for i in range(middle):
        lows.append(advance(i, lows[-1]))
        highs.append(advance(middle + i, highs[-1]))
        high_ends.append(retreat(BLOCKS - 1 - i, high_ends[-1]))
        low_ends.append(retreat(middle - 1 - i, low_ends[-1]))

    def joined_states(later_states, entry_state):
        moved = [mm(one[:, DV:], entry_state) for one in later_states]
        return [
            one + jnp.concatenate([later_one[:, :DV], nothing], 1)
            for one, later_one in zip(moved, later_states)
        ]

    forwards = lows[:middle] + joined_states(highs, lows[middle])
    backwards = high_ends[:middle] + joined_states(low_ends, high_ends[middle])
    for i in each:
        other = BLOCKS - 1 - i
        prefix_free_ref[i] = forwards[i][:, :DV].astype(bf16)
        prefix_ref[i] = forwards[i][:, DV:].astype(bf16)
        suffix_free_ref[other] = backwards[i][:, :DV].astype(bf16)
        suffix_ref[other] = backwards[i][:, DV:].astype(bf16)
    forward, backward = forwards[BLOCKS], backwards[BLOCKS]
    for k in range(8, HELD):
        copies[k].start()
    total = forward[:, DV:].astype(bf16)
    for other in range(SHARDS):
        send_ref[other, :DK] = total
        send_ref[other, DK:] = jnp.where(
            ints_ref[0] < other, forward[:, :DV], backward[:, :DV]
        ).astype(bf16)
    for copy in copies:
        copy.wait()


def tables(ints, floats, received):
    half = pltpu.HBM((BLOCKS, DK, DV), bf16)
    vmem = pl.BlockSpec(memory_space=pltpu.VMEM)
    smem = pl.BlockSpec(memory_space=pltpu.SMEM)
    return pl.pallas_call(
        tables_kernel,
        in_specs=[smem, smem, vmem],
        out_specs=[vmem] * 3 + [pl.BlockSpec(memory_space=pl.ANY)] * HELD,
        out_shape=[
            jax.ShapeDtypeStruct((SHARDS, 2 * DK, DV), bf16),
            pltpu.HBM((3, BLOCKS, 128), f32),
            pltpu.HBM((2, 128, 128), f32),
            *[half] * HELD,
        ],
        scratch_shapes=[pltpu.VMEM((BLOCKS, DK, DV), bf16)] * HELD
        + [pltpu.SemaphoreType.DMA((HELD,))],
        compiler_params=pltpu.CompilerParams(vmem_limit_bytes=SMALL_VMEM),
        cost_estimate=cost(30),
        name="tables",
    )(ints, floats, received)


def later_kernel(x_ref, inverse_ref, mixing_ref, keys_last_ref, fresh_ref, out_ref, push_ref, back_ref):
    each = range(LATER_BLOCKS)
    turned = [mm_tn(mixing_ref[i], block_rows(x_ref, i, 3)).astype(bf16) for i in each]
    outputs = [mm(mixing_ref[i], fresh_ref[i]) for i in each]
    pushed = [
        mm_tn(inverse_ref[i], jnp.concatenate([turned[i], keys_last_ref[i]], 1)).astype(bf16)
        for i in each
    ]
    for i in each:
        out_ref[i] = outputs[i].astype(bf16)
        push_ref[i] = pushed[i][:, :DV]
        back_ref[i] = pushed[i][:, DV:]


def later(received, inverse, mixing, keys_last, fresh):
    half = pltpu.HBM((BLOCKS, DK, DV), bf16)
    by_step = stepped(LATER_BLOCKS, GROUP, DV)
    return pl.pallas_call(
        later_kernel,
        grid=(BLOCKS // LATER_BLOCKS,),
        in_specs=[stepped(2 * LATER_BLOCKS, 256 + GATE_ROWS, 128)] + [by_step] * 4,
        out_specs=[by_step] * 3,
        out_shape=[half] * 3,
        compiler_params=pltpu.CompilerParams(vmem_limit_bytes=LARGE_VMEM),
        cost_estimate=cost(4),
        name="later",
    )(received, inverse, mixing, keys_last, fresh)


def split_two(state):
    high = state.astype(bf16)
    return jnp.concatenate([high, (state - high.astype(f32)).astype(bf16)], 1)


def gradients_kernel(
    ints_ref,
    x_ref,
    shards_ref,
    gate_ref,
    column_ref,
    out_ref,
    push_ref,
    back_ref,
    weighted_ref,
    strict_ref,
    mixing_ref,
    fresh_ref,
    seen_ref,
    read_ref,
    prefix_ref,
    prefix_free_ref,
    suffix_ref,
    suffix_free_ref,
    y_ref,
    ends_ref,
):
    here = pl.program_id(0)

    @pl.when(here == 0)
    def prologue():
        me = ints_ref[0]
        eye = eye_of(DK)
        nothing = jnp.zeros((DK, DV), f32)

        def step(at, used, turned, pair):
            low = pair.astype(bf16)
            rest = (pair - low.astype(f32)).astype(bf16)
            product = mm_tn if turned else mm
            moved = product(shards_ref[at, :DK], low) + product(shards_ref[at, :DK], rest)
            added = shards_ref[at, DK:].astype(f32)
            width = pair.shape[1]
            if width > DV:
                added = jnp.concatenate([added, jnp.zeros((DK, width - DV), f32)], 1)
            return jnp.where(used, moved + added, pair)

        early, late = nothing, jnp.concatenate([nothing, eye], 1)
        early_end, late_end = nothing, late
        for k in range(4):
            early = step(k, k < me, False, early)
            early_end = step(7 - k, 7 - k > me, True, early_end)
            if k < 3:
                late = step(4 + k, 4 + k < me, False, late)
                late_end = step(3 - k, 3 - k > me, True, late_end)

        def joined(late, early):
            moved = mm(late[:, DV:], split_two(early))
            return late[:, :DV] + moved[:, :DV] + moved[:, DV:]

        state = joined(late, early)
        adjoint = joined(late_end, early_end)
        ends_ref[0] = state.astype(bf16)
        ends_ref[1] = adjoint.astype(bf16)

    lane = iota((GROUP, 8), 1)
    sublane = iota((8, GROUP), 0)
    change_cols = jnp.zeros((GROUP, 8), f32)
    beta_cols = jnp.zeros((GROUP, 8), f32)
    column_sums = jnp.zeros((8, GROUP), f32)
    each = range(GRADIENT_BLOCKS)
    row, col = iota((GROUP, GROUP), 0), iota((GROUP, GROUP), 1)
    states = [prefix_free_ref[i].astype(f32) + mm(prefix_ref[i], ends_ref[0]) for i in each]
    adjoints = [suffix_free_ref[i].astype(f32) + mm(suffix_ref[i], ends_ref[1]) for i in each]
    states_low = [one.astype(bf16) for one in states]
    adjoints_low = [one.astype(bf16) for one in adjoints]
    fresh = [
        (fresh_ref[i].astype(f32) - mm(seen_ref[i], states_low[i])).astype(bf16) for i in each
    ]
    outputs = [out_ref[i].astype(f32) + mm(read_ref[i], states_low[i]) for i in each]
    pushed = [push_ref[i].astype(f32) + mm(back_ref[i], adjoints_low[i]) for i in each]
    norms = [normed(x_ref, i) for i in each]
    sides = [
        jnp.concatenate([block_rows(x_ref, i, 3), pushed[i].astype(bf16)], 0) for i in each
    ]
    on_fresh = [mm_nt(sides[i], fresh[i]) for i in each]
    on_state = [mm_nt(sides[i], states_low[i]) for i in each]
    on_adjoint = [mm_nt(fresh[i], adjoints_low[i]) for i in each]
    mix_terms = [weighted_ref[i].astype(f32) * on_fresh[i][:GROUP] for i in each]
    key_terms = [
        jnp.where(row > col, -weighted_ref[i].astype(f32) * on_fresh[i][GROUP:], 0.0) for i in each
    ]
    stacked = [
        jnp.concatenate([mix_terms[i].astype(bf16), key_terms[i].astype(bf16)], 0) for i in each
    ]
    direct = [mm(stacked[i], norms[i][5]) for i in each]
    turned = [
        mm_tn(stacked[i], jnp.concatenate([norms[i][4], norms[i][5]], 0)) for i in each
    ]
    for local in each:
        block = here * GRADIENT_BLOCKS + local
        entry, last = pick_column(column_ref[0], block), pick_column(column_ref[1], block)
        query_raw, key_raw, query_root, key_root, query, keys = norms[local]
        query_entry = entry * on_state[local][:GROUP]
        key_entry = -entry * on_state[local][GROUP:]
        key_last = last * on_adjoint[local]
        query_grad = query_entry + direct[local][:GROUP]
        key_grad = key_entry + key_last + direct[local][GROUP:] + turned[local]
        query_wide, key_wide = query.astype(f32), keys.astype(f32)
        table = (
            on_fresh[local][:GROUP] * mixing_ref[local].astype(f32)
            - on_fresh[local][GROUP:] * strict_ref[local].astype(f32)
        )
        last_sums = jnp.sum(key_wide * key_last, axis=1, keepdims=True)
        change = (
            jnp.sum(table + query_wide * query_entry + key_wide * key_entry, axis=1, keepdims=True)
            - last_sums
        )
        extra = jnp.sum(last_sums, axis=0, keepdims=True) + entry[GROUP - 1 :, :] * jnp.sum(
            jnp.sum(adjoints[local] * states[local], axis=0, keepdims=True), axis=1, keepdims=True
        )
        change = change + jnp.where(iota((GROUP, 1), 0) == GROUP - 1, extra, 0.0)
        change_cols = jnp.where(lane == local, change, change_cols)
        beta_cols = jnp.where(lane == local, last_sums, beta_cols)
        column_sums = jnp.where(
            sublane == local, jnp.sum(table, axis=0, keepdims=True), column_sums
        )
        query_grad = query_grad * DK ** (-0.5)
        query_dot = jnp.sum(query_grad * query_raw, axis=1, keepdims=True)
        key_dot = jnp.sum(key_grad * key_raw, axis=1, keepdims=True)
        query_back = query_root * query_grad - query_raw * (
            query_root * query_root * query_root * query_dot
        )
        key_back = key_root * key_grad - key_raw * (key_root * key_root * key_root * key_dot)
        for half in range(2):
            rows = slice(64 * half, 64 * half + 64)
            at = 2 * local + half
            y_ref[at, 0:64, :] = outputs[local][rows].astype(bf16)
            y_ref[at, 64:128, :] = query_back[rows].astype(bf16)
            y_ref[at, 128:192, :] = key_back[rows].astype(bf16)
            y_ref[at, 192:256, :] = pushed[local][rows].astype(bf16)

    after = jnp.where(row >= col, 1.0, 0.0)
    eye = jnp.where(row == col, 1.0, 0.0)
    decay_rows = exact(change_cols, after, 0, 0) - exact(column_sums, after, 1, 0)
    beta_rows = exact(beta_cols, eye, 0, 0) + column_sums
    for local in range(GRADIENT_BLOCKS):
        block = here * GRADIENT_BLOCKS + local
        decay_grad = decay_rows[local : local + 1] * gate_ref[2, pl.ds(block, 1), :]
        beta_grad = beta_rows[local : local + 1] * (1.0 - gate_ref[1, pl.ds(block, 1), :])
        rows = iota((GATE_ROWS, 128), 0)
        tail = jnp.where(rows == 0, decay_grad, jnp.where(rows == 1, beta_grad, 0.0)).astype(bf16)
        for half in range(2):
            y_ref[2 * local + half, 256:, :] = tail


def gradients(ints, received, shards, gate, column, *made):
    by_step = stepped(GRADIENT_BLOCKS, GROUP, DV)
    rows_spec = stepped(2 * GRADIENT_BLOCKS, 256 + GATE_ROWS, 128)
    return pl.pallas_call(
        gradients_kernel,
        grid=(BLOCKS // GRADIENT_BLOCKS,),
        in_specs=[
            pl.BlockSpec(memory_space=pltpu.SMEM),
            rows_spec,
            whole(SHARDS, 2 * DK, DV),
            whole(3, BLOCKS, 128),
            whole(2, 128, 128),
            *[by_step] * 13,
        ],
        out_specs=rows_spec,
        out_shape=jax.ShapeDtypeStruct(received.shape, bf16),
        scratch_shapes=[pltpu.VMEM((2, DK, DV), bf16)],
        compiler_params=pltpu.CompilerParams(
            dimension_semantics=("arbitrary",), vmem_limit_bytes=GRADIENT_VMEM
        ),
        cost_estimate=cost(20),
        name="gradients",
    )(ints, received, shards, gate, column, *made)


def pack_kernel(query_ref, key_ref, value_ref, decay_ref, beta_ref, grad_ref, x_ref):
    decay = jnp.concatenate([decay_ref[...].astype(f32)] * 2, 1)
    beta = jnp.concatenate([beta_ref[...].astype(f32)] * 2, 1)
    rows = iota((GATE_ROWS, 128), 0)
    for head in range(PACK_HEADS):
        shared = slice(DK * (head // 2), DK * (head // 2) + DK)
        own = slice(DV * head, DV * head + DV)
        x_ref[head, 0:64, :] = query_ref[:, shared]
        x_ref[head, 64:128, :] = key_ref[:, shared]
        x_ref[head, 128:192, :] = value_ref[:, own]
        x_ref[head, 192:256, :] = grad_ref[:, own]
        x_ref[head, 256:, :] = jnp.where(
            rows == 0,
            decay[head : head + 1],
            jnp.where(rows == 1, beta[head : head + 1], 0.0),
        ).astype(bf16)


def pack(query, key, value, decay, beta, grad):
    wide = pl.BlockSpec((64, PACK_HEADS * DV), lambda i: (0, i))
    narrow = pl.BlockSpec((64, PACK_HEADS * DK // 2), lambda i: (0, i))
    gates = pl.BlockSpec((PACK_HEADS, 64), lambda i: (i, 0))
    return pl.pallas_call(
        pack_kernel,
        grid=(VALUE_HEAD_COUNT // PACK_HEADS,),
        in_specs=[narrow, narrow, wide, gates, gates, wide],
        out_specs=pl.BlockSpec((PACK_HEADS, 256 + GATE_ROWS, 128), lambda i: (i, 0, 0)),
        out_shape=jax.ShapeDtypeStruct((VALUE_HEAD_COUNT, 256 + GATE_ROWS, 128), bf16),
        compiler_params=pltpu.CompilerParams(vmem_limit_bytes=LARGE_VMEM),
        name="pack",
    )(query, key, value, decay, beta, grad)


def unpack_kernel(ints_ref, y_ref, out_ref, query_ref, key_ref, value_ref, decay_ref, beta_ref):
    for head in range(PACK_HEADS):
        own = slice(DV * head, DV * head + DV)
        out_ref[:, own] = y_ref[head, 0:64, :]
        value_ref[:, own] = y_ref[head, 192:256, :]
    for head in range(PACK_HEADS // 2):
        shared = slice(DK * head, DK * head + DK)
        for part, ref in ((1, query_ref), (2, key_ref)):
            rows = slice(64 * part, 64 * part + 64)
            summed = y_ref[2 * head, rows, :].astype(f32) + y_ref[2 * head + 1, rows, :].astype(f32)
            ref[:, shared] = summed.astype(bf16)
    tail = y_ref[:, 256:, :].astype(f32)
    rows = iota(tail.shape, 1)
    for index, ref in ((0, decay_ref), (1, beta_ref)):
        picked = jnp.sum(jnp.where(rows == index, tail, 0.0), axis=1)
        ref[...] = jnp.where(ints_ref[5] == 0, picked[:, :64], picked[:, 64:]).astype(bf16)


def unpack(ints, returned):
    wide = pl.BlockSpec((64, PACK_HEADS * DV), lambda i: (0, i))
    narrow = pl.BlockSpec((64, PACK_HEADS * DK // 2), lambda i: (0, i))
    gates = pl.BlockSpec((PACK_HEADS, 64), lambda i: (i, 0))
    wide_out = jax.ShapeDtypeStruct((64, VALUE_HEAD_COUNT * DV), bf16)
    narrow_out = jax.ShapeDtypeStruct((64, NK * DK), bf16)
    gates_out = jax.ShapeDtypeStruct((VALUE_HEAD_COUNT, 64), bf16)
    return pl.pallas_call(
        unpack_kernel,
        grid=(VALUE_HEAD_COUNT // PACK_HEADS,),
        in_specs=[
            pl.BlockSpec(memory_space=pltpu.SMEM),
            pl.BlockSpec((PACK_HEADS, 256 + GATE_ROWS, 128), lambda i: (i, 0, 0)),
        ],
        out_specs=[wide, narrow, narrow, wide, gates, gates],
        out_shape=[wide_out, narrow_out, narrow_out, wide_out, gates_out, gates_out],
        compiler_params=pltpu.CompilerParams(vmem_limit_bytes=SMALL_VMEM),
        name="unpack",
    )(ints, returned)


def local(
    query_raw,
    key_raw,
    value_raw,
    decay_raw,
    beta_raw,
    decay_base,
    decay_bias,
    doc_lengths,
    out_grad,
):
    head = lax.axis_index("head")
    shard = lax.axis_index("ctx")
    sent = pack(query_raw, key_raw, value_raw, decay_raw.T, beta_raw.T, out_grad)
    received = lax.all_to_all(sent, "head", split_axis=0, concat_axis=0, tiled=True)
    ends = [jnp.sum(doc_lengths[:j]) for j in range(4)]
    ints = jnp.stack([shard.astype(jnp.int32), *ends, (head % 2).astype(jnp.int32)])
    floats = jnp.stack(
        [
            lax.dynamic_index_in_dim(decay_base, head, keepdims=False),
            lax.dynamic_index_in_dim(decay_bias, head, keepdims=False),
        ]
    )
    send, gate, column, weighted, strict, mixing, inverse, keys_last, fresh, *made = tables(
        ints, floats, received
    )
    shards = lax.all_to_all(send, "ctx", split_axis=0, concat_axis=0, tiled=True)
    out, push, turned = later(received, inverse, mixing, keys_last, fresh)
    back = gradients(
        ints, received, shards, gate, column, out, push, turned, weighted, strict, mixing, fresh, *made
    )
    returned = lax.all_to_all(back, "head", split_axis=0, concat_axis=0, tiled=True)
    output, query_grad, key_grad, value_grad, decay_grad, beta_grad = unpack(ints, returned)
    return (output, query_grad, key_grad, value_grad, decay_grad.T, beta_grad.T)


def solution(mesh):
    placed = (
        P(("ctx", "head"), None),
        P(("ctx", "head"), None),
        P(("ctx", "head"), None),
        P(("ctx", "head"), None),
        P(("ctx", "head"), None),
        P(),
        P(),
        P(),
        P(("ctx", "head"), None),
    )
    return jax.shard_map(
        local,
        mesh=mesh,
        in_specs=placed,
        out_specs=(P(("ctx", "head"), None),) * 6,
        check_vma=False,
    )
```
